512 devices in a mesh: ctx: 16 (over z), dp: 4 (over y_hi, core), tp: 8 (over y_lo, x).
Axes of the slice: x: 4, y: 4 (y_hi: 2, y_lo: 2; y = y_hi * 2 + y_lo), z: 16, core: 2. Of those that a mesh axis runs over, the one named last changes fastest.
Arguments:
- queries: bfloat16 [4, 16, 320, 3072], P('dp', 'ctx', None, 'tp'), may hold values from -8 to 8
- keys: bfloat16 [4, 16, 320, 3072], P('dp', 'ctx', None, 'tp'), may hold values from -8 to 8
- values: bfloat16 [4, 16, 320, 3072], P('dp', 'ctx', None, 'tp'), may hold values from -6 to 6
- out_grad: bfloat16 [4, 16, 320, 2560], P('dp', 'ctx', None, 'tp'), may hold values from -6 to 6
- out_weight: bfloat16 [2560, 3072], P('dp', 'tp'), may hold values from -0.109375 to 0.109375
- short_docs: int32 [4, 16, 256], P('dp', 'ctx'), may hold values from 0 to 7, never falling along the last dimension, each value on 1 to 128 neighbouring positions
- long_docs: int32 [4, 1024], P('dp'), may hold values from 0 to 1, never falling along the last dimension, each value on 1 to 768 neighbouring positions
- block_place: int32 [4, 16], P('dp'), may hold values from 0 to 15, each once within a row
Outputs:
- query_grad: bfloat16 [4, 16, 320, 3072], P('dp', 'ctx', None, 'tp')
- key_grad: bfloat16 [4, 16, 320, 3072], P('dp', 'ctx', None, 'tp')
- value_grad: bfloat16 [4, 16, 320, 3072], P('dp', 'ctx', None, 'tp')
- weight_grad: float32 [2560, 3072], P(('ctx', 'dp'), 'tp')
The draws below stay inside these ranges and needn't reach their ends.
Inputs may be any that keep to these rules, and one draw needn't show every extreme that they name: `short_docs`: never falling along the 256 tokens, each document 1 to 128 tokens. `long_docs`: never falling along the 1024 positions, each document 1 to 768 positions. `block_place`: each row a permutation.
All inputs are finite; a program needn't handle non-finite values.
Results may differ from the reference program's by a relative error of at most 0.025.
Values may be sent and summed in bfloat16 or wider, within the bound.
A program may use at most 64 MiB of HBM per device.

```python
import math
import jax
import jax.numpy as jnp
import numpy as np
from jax import lax

HEADS = 24
HD = 128
DOUT = 2560
LOC = 256
BLK = 64
ROWS = 320
LONG = 1024
WINDOWS = 4
FEATS = 3072
N_CTX = 16


def pattern(key):
    signs = jnp.where(jax.random.bernoulli(key, 0.5, (WINDOWS, LONG // BLK, ROWS, FEATS)), 1.0, -1.0)
    return signs


def draw_queries(key, part):
    signs = pattern(key)
    key = jax.random.fold_in(key, 11)
    shape = signs.shape
    base = jnp.clip(jax.random.normal(key, shape, jnp.float32), -6.0, 6.0)
    return base.astype(jnp.bfloat16)


def draw_keys(key, part):
    signs = pattern(key)
    key = jax.random.fold_in(key, 13)
    shape = signs.shape
    base = jnp.clip(jax.random.normal(key, shape, jnp.float32), -6.0, 6.0)
    return base.astype(jnp.bfloat16)


def spiked(result, key, source, target, shards_of, factor):
    def block_of(dim):
        return (jnp.arange(result.shape[dim]) // (result.shape[dim] // shards_of)).reshape((-1,) + (1,) * (result.ndim - 1 - dim))

    near = jax.random.permutation(key, shards_of)[block_of(target)]
    second = (block_of(target) + shards_of // 2) % shards_of
    return jnp.where((block_of(source) == near) | (block_of(source) == second), factor * result, result)


def block_levels(rng, dims, split, least, largest):
    def one(position, blocks):
        heights = jax.random.uniform(jax.random.fold_in(jax.random.fold_in(rng, 6), position), (blocks,), jnp.float32, least / len(split), largest / len(split))
        return jnp.repeat(jnp.exp(heights), dims[position] // blocks).reshape((-1,) + (1,) * (len(dims) - position - 1))

    loudness = one(*split[0])
    for cut in split[1:]:
        loudness = loudness * one(*cut)
    return loudness


def profile(number_of, total, bound, lean):
    weights = [(1 << 20) // math.isqrt(grade ** lean) + 1 for grade in range(2, number_of + 1)]
    rest, given = total - bound - (number_of - 1), [1] * (number_of - 1)
    while rest > 0:
        candidates = [i for i in range(number_of - 1) if given[i] < bound]
        whole, left = sum([weights[i] for i in candidates]), rest
        for i in candidates:
            addition = min(bound - given[i], max(1, left * weights[i] // whole), rest)
            given[i] = given[i] + addition
            rest = rest - addition
    return np.array([bound] + given)


def uneven(own_key, count, total, limit, skew):
    if count == 2:
        one = jax.random.randint(own_key, (), max(1, total - limit), min(limit, total - 1) + 1)
        return jnp.stack([one, total - one])
    sizes = jnp.asarray(profile(count, total, limit, skew), jnp.int32)
    twos = (count - 1) // 2
    donor, taker = sizes[1:1 + 2 * twos:2], sizes[2:2 + 2 * twos:2]
    slack = jnp.minimum(donor - 1, limit - taker)
    moved = jax.random.randint(jax.random.fold_in(own_key, 1), (twos,), 0, 1 << 20) % (slack + 1)
    sizes = sizes.at[1:1 + 2 * twos:2].set(donor - moved).at[2:2 + 2 * twos:2].set(taker + moved)
    return sizes[jax.random.permutation(jax.random.fold_in(own_key, 2), count)]


def noise(key, extent, deviation, most, shards=(), kind=jnp.bfloat16):
    values = jax.random.normal(key, extent, jnp.float32) * deviation
    if len(shards) > 0:
        values = block_levels(key, extent, shards, -0.22, 0.18) * values
    return jnp.clip(values, min=-most, max=most).astype(kind)


def bell_draw_with(stream_key, shape, width, most, pieces, heavy, kind=jnp.bfloat16):
    values = width * jax.random.normal(stream_key, shape, jnp.float32)
    if pieces:
        values = values * block_levels(stream_key, shape, pieces, -0.22, 0.18)
    return jnp.clip(spiked(values, jax.random.fold_in(stream_key, 3), *heavy), -most, most).astype(kind)


def setup_inputs(seed: int = 0) -> dict:
    seeds = jax.random.split(jax.random.key(seed), 9)
    return {
        "queries": draw_queries(jax.random.fold_in(seeds[8], 71), 0),
        "keys": draw_keys(jax.random.fold_in(seeds[8], 71), 0),
        "values": noise(seeds[2], (WINDOWS, N_CTX, ROWS, FEATS), 1.0, 6.0, ((0, 4), (1, 16), (3, 8))),
        "out_grad": bell_draw_with(seeds[3], (WINDOWS, N_CTX, ROWS, DOUT), 1.0, 6.0, ((0, 4), (1, 16), (3, 8)), (1, 3, 16, 2.0)),
        "out_weight": noise(seeds[4], (DOUT, FEATS), FEATS ** -0.5, 0.109375, ((0, 4), (1, 8))),
        "short_docs": jax.vmap(lambda own: jnp.searchsorted(jnp.cumsum(uneven(own, max(LOC // 32, 3), LOC, LOC // 2, 2)), jnp.arange(LOC), side="right"))(jax.random.split(seeds[5], WINDOWS * N_CTX)).reshape((WINDOWS, N_CTX, LOC)).astype(jnp.int32),
        "long_docs": jax.vmap(lambda own: jnp.searchsorted(jnp.cumsum(uneven(own, 2, LONG, LONG * 3 // 4, 2)), jnp.arange(LONG), side="right"))(jax.random.split(seeds[6], WINDOWS)).reshape((WINDOWS, LONG)).astype(jnp.int32),
        "block_place": jax.vmap(lambda own: jax.random.permutation(own, N_CTX))(jax.random.split(seeds[7], WINDOWS)).reshape((WINDOWS, N_CTX)).astype(jnp.int32),
    }


NEG = -1e30


def attend_head(query, key, value, grad, mask):
    scale = HD ** -0.5
    qf = query.astype(jnp.float32)
    kf = key.astype(jnp.float32)
    vf = value.astype(jnp.float32)
    gf = grad.astype(jnp.float32)
    scores = jnp.dot(qf, kf.T) * scale
    scores = jnp.where(mask, scores, NEG)
    top = jnp.max(scores, axis=1, keepdims=True)
    lse = top + jnp.log(jnp.sum(jnp.exp(scores - top), axis=1, keepdims=True))
    prob = jnp.where(mask, jnp.exp(scores - lse), 0.0)
    weights = lax.optimization_barrier(prob.astype(jnp.bfloat16))
    wf = weights.astype(jnp.float32)
    attn = jnp.dot(wf, vf).astype(jnp.bfloat16)
    delta = jnp.sum(gf * attn.astype(jnp.float32), axis=1, keepdims=True)
    dpv = jnp.dot(gf, vf.T)
    dsc = lax.optimization_barrier((prob * (dpv - delta)).astype(jnp.bfloat16)).astype(jnp.float32)
    dq = (jnp.dot(dsc, kf) * scale).astype(jnp.bfloat16)
    dk = (jnp.dot(dsc.T, qf) * scale).astype(jnp.bfloat16)
    dv = jnp.dot(wf.T, gf).astype(jnp.bfloat16)
    return attn, dq, dk, dv


def split_heads(block):
    return block.reshape(block.shape[0], HEADS, HD).transpose(1, 0, 2)


def join_heads(block):
    return block.transpose(1, 0, 2).reshape(block.shape[1], HEADS * HD)


def region(query, key, value, grad, mask):
    outs = lax.map(lambda t: attend_head(t[0], t[1], t[2], t[3], mask),
                   (split_heads(query), split_heads(key), split_heads(value), split_heads(grad)))
    return tuple(join_heads(piece) for piece in outs)


def window(query, key, value, cotangent, out_weight, short_ids, long_ids, place):
    grad = jnp.dot(cotangent.reshape(-1, DOUT), out_weight, preferred_element_type=jnp.float32)
    grad = grad.astype(jnp.bfloat16).reshape(N_CTX, ROWS, HEADS * HD)
    spots = jnp.arange(LOC)

    def short_one(t):
        mask = (spots[None, :] <= spots[:, None]) & (t[4][None, :] == t[4][:, None])
        return region(t[0], t[1], t[2], t[3], mask)

    short = lax.map(short_one, (query[:, :LOC], key[:, :LOC], value[:, :LOC], grad[:, :LOC], short_ids))

    def to_long(block):
        empty = jnp.zeros((N_CTX, BLK, HEADS * HD), block.dtype)
        return empty.at[place].set(block[:, LOC:]).reshape(LONG, HEADS * HD)

    lpos = jnp.arange(LONG)
    lmask = (lpos[None, :] <= lpos[:, None]) & (long_ids[None, :] == long_ids[:, None])
    longs = region(to_long(query), to_long(key), to_long(value), to_long(grad), lmask)
    back = [piece.reshape(N_CTX, BLK, HEADS * HD)[place] for piece in longs]
    full = [jnp.concatenate([a, b], axis=1) for a, b in zip(short, back)]
    term = jnp.dot(cotangent.reshape(-1, DOUT).T, full[0].reshape(-1, HEADS * HD),
                   preferred_element_type=jnp.float32)
    return full[1], full[2], full[3], term


def reference(queries, keys, values, out_grad, out_weight, short_docs, long_docs, block_place):
    def one(t):
        return window(t[0], t[1], t[2], t[3], out_weight, t[4], t[5], t[6])

    dq, dk, dv, terms = lax.map(one, (queries, keys, values, out_grad, short_docs, long_docs, block_place))
    return dq, dk, dv, jnp.sum(terms, axis=0)
```

```python
import math

import jax
import jax.numpy as jnp
from jax import lax
from jax.experimental import pallas as pl
from jax.experimental.pallas import tpu as pltpu
from jax.sharding import PartitionSpec as P

HD = 128
LOC = 256
BLK = 64
NEG = -1e30
MESH = pl.DeviceIdType.MESH
F32 = jnp.float32
BF16 = jnp.bfloat16
SCALE = HD**-0.5
C2 = SCALE * math.log2(math.e)


def nn(a, b):
    return lax.dot_general(a, b, (((1,), (0,)), ((), ())), preferred_element_type=F32)


def nt(a, b):
    return lax.dot_general(a, b, (((1,), (1,)), ((), ())), preferred_element_type=F32)


def softmax_t(scores, mask):
    s = jnp.where(mask, scores * C2, NEG)
    top = jnp.max(s, axis=0, keepdims=True)
    p = jnp.exp2(s - top)
    return p * (1.0 / jnp.sum(p, axis=0, keepdims=True))


def kernel(
    q_ref, k_ref, v_ref, og_ref, w_ref, sdoc_ref, ldoc_ref, place_ref,
    dq_ref, dk_ref, dv_ref, wg_ref,
    og_full, w_full, w_tr, stage, gstage, hot_in, hot_g, hot_p, hot_at, hot_attn, hot_grads, hot_acc,
    attn_in, grads_in, attn_all, attn_t, p_short, g_all, part, half_out, half_in,
    down_out, down_in, up_out, up_in, red, last_out, last_in,
    og_s, og_r, w_s, w_r, st_s, gs_s, hin_r, hg_r, ha_s, at_r, ho_s, gr_r,
    half_s, half_r, dn_s, dn_r, up_s, up_r, last_s, last_r,
):
    z = lax.axis_index("ctx")
    dp = lax.axis_index("dp")
    tp = lax.axis_index("tp")
    nz = 16
    y_hi, core = dp // 2, dp % 2
    y_lo, x = tp // 4, tp % 4
    row, other = y_lo * 4, (1 - y_lo) * 4
    xr, xl, xo = (x + 1) % 4, (x + 3) % 4, (x + 2) % 4
    dpo = (1 - y_hi) * 2 + core
    sib = y_hi * 2 + 1 - core
    right, left = {"tp": row + xr}, {"tp": row + xl}
    pair = {"tp": other + x}
    cross = {"dp": dpo, "tp": other + x}
    opposite = {"dp": dpo}
    sibling = {"dp": sib}
    zup, zdn = {"ctx": (z + 1) % nz}, {"ctx": (z + nz - 1) % nz}
    rel = (z + nz - 3 * core) % nz
    is_hot = (rel % 5 == 0) & (rel < 15)
    hot_h = rel // 5

    def rc(src, dst, ss, rs, dev):
        return pltpu.make_async_remote_copy(
            src_ref=src, dst_ref=dst, send_sem=ss, recv_sem=rs, device_id=dev, device_id_type=MESH
        )

    bar = pltpu.get_barrier_semaphore()
    for dev in (right, left, pair, cross, opposite, sibling):
        pl.semaphore_signal(bar, inc=1, device_id=dev, device_id_type=MESH)

    def greet(i, carry):
        pl.semaphore_signal(bar, inc=1, device_id={"ctx": (z + i) % nz}, device_id_type=MESH)
        return carry

    lax.fori_loop(1, nz, greet, 0)

    for h in range(3):
        hs = slice(h * HD, (h + 1) * HD)
        stage[h, 0] = q_ref[LOC:, hs]
        stage[h, 1] = k_ref[LOC:, hs]
        stage[h, 2] = v_ref[LOC:, hs]
    og_full[tp] = og_ref[...]
    w_full[dp] = w_ref[...]
    pl.semaphore_wait(bar, 21)

    lo, hi = pl.ds(0, 160), pl.ds(160, 160)
    wlo, whi = pl.ds(0, 320), pl.ds(320, 320)
    og = [
        (og_ref, og_full.at[tp], right, og_full.at[row + xl]),
        (og_ref, og_full.at[tp], left, og_full.at[row + xr]),
        (og_ref, og_full.at[tp], pair, og_full.at[other + x]),
        (og_full.at[row + xl, lo], og_full.at[row + xl, lo], right, og_full.at[row + xo, lo]),
        (og_full.at[row + xr, hi], og_full.at[row + xr, hi], left, og_full.at[row + xo, hi]),
        (og_full.at[other + x], og_full.at[other + x], right, og_full.at[other + xl]),
        (og_full.at[other + x], og_full.at[other + x], left, og_full.at[other + xr]),
        (og_full.at[other + xl, lo], og_full.at[other + xl, lo], right, og_full.at[other + xo, lo]),
        (og_full.at[other + xr, hi], og_full.at[other + xr, hi], left, og_full.at[other + xo, hi]),
    ]
    wg = [
        (w_ref.at[wlo], w_tr.at[0], pair, w_tr.at[0]),
        (w_ref.at[whi], w_tr.at[1], cross, w_tr.at[1]),
        (w_ref, w_full.at[dp], sibling, w_full.at[sib]),
        (w_tr.at[0], w_full.at[dp, wlo], cross, w_full.at[dpo, wlo]),
        (w_tr.at[1], w_full.at[dpo, whi], pair, w_full.at[dpo, whi]),
        (w_full.at[dpo, wlo], w_full.at[dpo, wlo], sibling, w_full.at[(1 - y_hi) * 2 + 1 - core, wlo]),
        (w_full.at[dpo, whi], w_full.at[dpo, whi], sibling, w_full.at[(1 - y_hi) * 2 + 1 - core, whi]),
    ]

    def og_go(i):
        src, dst, dev, _ = og[i]
        rc(src, dst, og_s.at[i], og_r.at[i], dev).start()

    def og_wait(i):
        land = og[i][3]
        rc(land, land, og_s.at[i], og_r.at[i], og[i][2]).wait_recv()

    def w_go(i):
        src, dst, dev, _ = wg[i]
        rc(src, dst, w_s.at[i], w_r.at[i], dev).start()

    def w_wait(i):
        land = wg[i][3]
        rc(land, land, w_s.at[i], w_r.at[i], wg[i][2]).wait_recv()

    for i in (2, 0, 1):
        og_go(i)
    for i in (0, 1, 2):
        w_go(i)

    def owner(h):
        return 5 * h + 3 * core

    def to_hot(h):
        return rc(stage.at[h], hot_in.at[z], st_s.at[h], hin_r.at[z], {"ctx": owner(h)})

    def g_to_hot(h):
        return rc(gstage.at[h], hot_g.at[z], gs_s.at[h], hg_r.at[z], {"ctx": owner(h)})

    for h in range(3):
        @pl.when(z != owner(h))
        def _():
            to_hot(h).start()

        @pl.when(z == owner(h))
        def _():
            hot_in[z] = stage[h]

    sid = sdoc_ref[...].astype(F32)
    sid_col = jnp.broadcast_to(sid, (HD, LOC)).T
    sid_col = jnp.concatenate([sid_col, sid_col], axis=1)
    kk = lax.broadcasted_iota(jnp.int32, (LOC, LOC), 0)
    qq = lax.broadcasted_iota(jnp.int32, (LOC, LOC), 1)
    smask = (kk <= qq) & (sid_col == sid)
    for h in range(3):
        hs = slice(h * HD, (h + 1) * HD)
        p = softmax_t(nt(k_ref[:LOC, hs], q_ref[:LOC, hs]), smask).astype(BF16)
        p_short[h] = p
        at = nn(v_ref[:LOC, hs].T, p).astype(BF16).astype(F32)
        attn_t[h] = at
        attn_all[:LOC, hs] = at.T.astype(BF16)

    og_wait(2)
    og_go(5)
    og_go(6)
    og_wait(0)
    og_go(3)
    og_wait(1)
    og_go(4)
    w_wait(0)
    w_go(3)
    w_wait(1)
    w_go(4)
    og_wait(5)
    og_go(7)
    og_wait(6)
    og_go(8)

    def each_other(fn):
        def body(i, carry):
            fn((z + i) % nz)
            return carry

        lax.fori_loop(1, nz, body, 0)

    def attn_back(c):
        return rc(hot_attn.at[c], attn_in.at[hot_h], ha_s.at[c], at_r.at[hot_h], {"ctx": c})

    def grads_back(c):
        return rc(hot_grads.at[c], grads_in.at[hot_h], ho_s.at[c], gr_r.at[hot_h], {"ctx": c})

    @pl.when(is_hot)
    def _():
        each_other(lambda c: rc(hot_in.at[c], hot_in.at[c], st_s.at[0], hin_r.at[c], zup).wait_recv())
        lane = lax.broadcasted_iota(jnp.int32, (1, 1024), 1)
        blk = lane // BLK
        place = jnp.zeros((1, 1024), jnp.int32)
        for c in range(nz):
            place = jnp.where(blk == c, place_ref[0, c], place)
        qpos = place * BLK + lane % BLK
        total = jnp.sum(ldoc_ref[...].astype(F32), axis=1, keepdims=True)
        cut = 1024 - total.astype(jnp.int32)
        qlo = jnp.where(qpos >= cut, cut, 0)
        k_all = hot_in[:, 1].reshape(1024, HD)
        v_t = hot_in[:, 2].reshape(1024, HD).T
        for t in range(4):
            ts = slice(t * 256, (t + 1) * 256)
            q_t = hot_in[4 * t : 4 * t + 4, 0].reshape(256, HD)
            s = nt(k_all, q_t)
            spot = lax.broadcasted_iota(jnp.int32, (BLK, 256), 0)
            kpos = jnp.concatenate([spot + place_ref[0, c] * BLK for c in range(nz)], axis=0)
            mask = (kpos <= qpos[:, ts]) & (kpos >= qlo[:, ts])
            p = softmax_t(s, mask).astype(BF16)
            hot_p[:, ts] = p
            at = nn(v_t, p).astype(BF16).astype(F32)
            hot_at[:, ts] = at
            hot_attn[4 * t : 4 * t + 4] = at.T.astype(BF16).reshape(4, BLK, HD)
        each_other(lambda c: attn_back(c).start())

    w_wait(3)
    w_go(5)
    w_wait(4)
    w_go(6)
    w_wait(2)
    og_wait(3)
    og_wait(4)
    og_wait(7)
    og_wait(8)
    w_wait(5)
    w_wait(6)

    acc = jnp.zeros((320, 384), F32)
    for t in range(8):
        acc += nn(og_full[t], w_full[t // 2, (t % 2) * 320 : (t % 2) * 320 + 320])
    g_all[...] = acc.astype(BF16)
    for h in range(3):
        gstage[h] = g_all[LOC:, h * HD : (h + 1) * HD]
    for h in range(3):
        @pl.when(z != owner(h))
        def _():
            g_to_hot(h).start()

        @pl.when(z == owner(h))
        def _():
            hot_g[z] = gstage[h]

    for h in range(3):
        hs = slice(h * HD, (h + 1) * HD)

        @pl.when(z != owner(h))
        def _():
            rc(attn_in.at[h], attn_in.at[h], gs_s.at[h], at_r.at[h], zup).wait_recv()
            attn_all[LOC:, hs] = attn_in[h]

        @pl.when(z == owner(h))
        def _():
            attn_all[LOC:, hs] = hot_attn[z]

    for t in range(8):
        w = nn(og_full[t].T, attn_all[...])
        for g in range(8):
            c, d = t * 2 + g // 4, g % 4
            part[d % 2, c, (d // 2) * 40 : (d // 2) * 40 + 40] = w[g * 40 : g * 40 + 40]
    half_out[...] = part[1 - core].astype(BF16)
    half = rc(half_out, half_in, half_s, half_r, sibling)
    half.start()

    for h in range(3):
        hs = slice(h * HD, (h + 1) * HD)
        g = g_all[:LOC, hs]
        v, k = v_ref[:LOC, hs], k_ref[:LOC, hs]
        delta = jnp.sum(g.T.astype(F32) * attn_t[h], axis=0, keepdims=True)
        p = p_short[h]
        ds = (p.astype(F32) * (nt(v, g) - delta)).astype(BF16)
        dk_ref[:LOC, hs] = (nn(ds, q_ref[:LOC, hs]) * SCALE).astype(BF16)
        dv_ref[:LOC, hs] = nn(p, g).astype(BF16)
        dq_ref[:LOC, hs] = (nn(k.T, ds).T * SCALE).astype(BF16)

    half.wait_recv()
    red[...] = part[core] + half_in[...].astype(F32)

    def hot_back(t):
        ts = slice(t * 256, (t + 1) * 256)
        if t == 0:
            each_other(lambda c: rc(hot_g.at[c], hot_g.at[c], gs_s.at[0], hg_r.at[c], zup).wait_recv())
        g = hot_g[4 * t : 4 * t + 4].reshape(256, HD)
        q = hot_in[4 * t : 4 * t + 4, 0].reshape(256, HD)
        delta = jnp.sum(g.T.astype(F32) * hot_at[:, ts], axis=0, keepdims=True)
        p = hot_p[:, ts]
        ds = (p.astype(F32) * (nt(hot_in[:, 2].reshape(1024, HD), g) - delta)).astype(BF16)
        dk = nn(ds, q)
        dv = nn(p, g)
        if t == 0:
            hot_acc[0] = dk
            hot_acc[1] = dv
        else:
            hot_acc[0] += dk
            hot_acc[1] += dv
        dq = nn(hot_in[:, 1].reshape(1024, HD).T, ds).T * SCALE
        hot_grads[4 * t : 4 * t + 4, 0] = dq.astype(BF16).reshape(4, BLK, HD)
        if t == 3:
            hot_grads[:, 1] = (hot_acc[0] * SCALE).astype(BF16).reshape(nz, BLK, HD)
            hot_grads[:, 2] = hot_acc[1].astype(BF16).reshape(nz, BLK, HD)
            each_other(lambda c: grads_back(c).start())

    def down(s):
        return rc(down_out.at[s], down_in.at[s], dn_s.at[s], dn_r.at[s], zdn)

    def up(s):
        return rc(up_out.at[s], up_in.at[s], up_s.at[s], up_r.at[s], zup)

    for s in range(8):
        v = red[(z + 8 + s) % nz]
        if s > 0:
            down(s - 1).wait_recv()
            v = v + down_in[s - 1].astype(F32)
        down_out[s] = v.astype(BF16)
        down(s).start()
        if s < 7:
            v = red[(z + 7 - s) % nz]
            if s > 0:
                up(s - 1).wait_recv()
                v = v + up_in[s - 1].astype(F32)
            up_out[s] = v.astype(BF16)
            up(s).start()
        if 1 <= s <= 4:
            pl.when(is_hot)(lambda: hot_back(s - 1))
    up(6).wait_recv()
    down(7).wait_recv()
    red[z] = red[z] + up_in[6].astype(F32) + down_in[7].astype(F32)
    last_out[0] = red[z, :40]
    last_out[1] = red[z, 40:]
    last = rc(last_out.at[1 - y_hi], last_in, last_s, last_r, opposite)
    last.start()

    for h in range(3):
        hs = slice(h * HD, (h + 1) * HD)

        @pl.when(z != owner(h))
        def _():
            rc(grads_in.at[h], grads_in.at[h], gs_s.at[h], gr_r.at[h], zup).wait_recv()
            dq_ref[LOC:, hs] = grads_in[h, 0]
            dk_ref[LOC:, hs] = grads_in[h, 1]
            dv_ref[LOC:, hs] = grads_in[h, 2]

        @pl.when(z == owner(h))
        def _():
            dq_ref[LOC:, hs] = hot_grads[z, 0]
            dk_ref[LOC:, hs] = hot_grads[z, 1]
            dv_ref[LOC:, hs] = hot_grads[z, 2]

    last.wait_recv()
    wg_ref[...] = last_out[y_hi] + last_in[...]

    for i in range(9):
        rc(og[i][0], og[i][1], og_s.at[i], og_r.at[i], og[i][2]).wait_send()
    for i in range(7):
        rc(wg[i][0], wg[i][1], w_s.at[i], w_r.at[i], wg[i][2]).wait_send()
    for h in range(3):
        @pl.when(z != owner(h))
        def _():
            to_hot(h).wait_send()
            g_to_hot(h).wait_send()

    @pl.when(is_hot)
    def _():
        each_other(lambda c: attn_back(c).wait_send())
        each_other(lambda c: grads_back(c).wait_send())

    half.wait_send()
    for s in range(8):
        down(s).wait_send()
        if s < 7:
            up(s).wait_send()
    last.wait_send()


def local(queries, keys, values, out_grad, out_weight, short_docs, long_docs, block_place):
    vm = pl.BlockSpec(memory_space=pltpu.VMEM)
    dma = pltpu.SemaphoreType.DMA
    dq, dk, dv, wg = pl.pallas_call(
        kernel,
        out_shape=(
            jax.ShapeDtypeStruct((320, 384), BF16),
            jax.ShapeDtypeStruct((320, 384), BF16),
            jax.ShapeDtypeStruct((320, 384), BF16),
            jax.ShapeDtypeStruct((40, 384), F32),
        ),
        in_specs=[vm] * 7 + [pl.BlockSpec(memory_space=pltpu.SMEM)],
        out_specs=(vm,) * 4,
        scratch_shapes=[
            pltpu.VMEM((8, 320, 320), BF16),
            pltpu.VMEM((4, 640, 384), BF16),
            pltpu.VMEM((2, 320, 384), BF16),
            pltpu.VMEM((3, 3, 64, 128), BF16),
            pltpu.VMEM((3, 64, 128), BF16),
            pltpu.VMEM((16, 3, 64, 128), BF16),
            pltpu.VMEM((16, 64, 128), BF16),
            pltpu.VMEM((1024, 1024), BF16),
            pltpu.VMEM((128, 1024), F32),
            pltpu.VMEM((16, 64, 128), BF16),
            pltpu.VMEM((16, 3, 64, 128), BF16),
            pltpu.VMEM((2, 1024, 128), F32),
            pltpu.VMEM((3, 64, 128), BF16),
            pltpu.VMEM((3, 3, 64, 128), BF16),
            pltpu.VMEM((320, 384), BF16),
            pltpu.VMEM((3, 128, 256), F32),
            pltpu.VMEM((3, 256, 256), BF16),
            pltpu.VMEM((320, 384), BF16),
            pltpu.VMEM((2, 16, 80, 384), F32),
            pltpu.VMEM((16, 80, 384), BF16),
            pltpu.VMEM((16, 80, 384), BF16),
            pltpu.VMEM((8, 80, 384), BF16),
            pltpu.VMEM((8, 80, 384), BF16),
            pltpu.VMEM((7, 80, 384), BF16),
            pltpu.VMEM((7, 80, 384), BF16),
            pltpu.VMEM((16, 80, 384), F32),
            pltpu.VMEM((2, 40, 384), F32),
            pltpu.VMEM((40, 384), F32),
            dma((9,)), dma((9,)), dma((7,)), dma((7,)),
            dma((3,)), dma((3,)), dma((16,)), dma((16,)),
            dma((16,)), dma((3,)), dma((16,)), dma((3,)),
            dma, dma, dma((8,)), dma((8,)), dma((7,)), dma((7,)), dma, dma,
        ],
        compiler_params=pltpu.CompilerParams(
            collective_id=0, has_side_effects=True, vmem_limit_bytes=50 * 1024 * 1024
        ),
        name="attention_grads",
    )(
        queries[0, 0], keys[0, 0], values[0, 0], out_grad[0, 0], out_weight,
        short_docs[0], long_docs, block_place,
    )
    shape = queries.shape
    return dq.reshape(shape), dk.reshape(shape), dv.reshape(shape), wg


def solution(mesh):
    placed = (
        P("dp", "ctx", None, "tp"),
        P("dp", "ctx", None, "tp"),
        P("dp", "ctx", None, "tp"),
        P("dp", "ctx", None, "tp"),
        P("dp", "tp"),
        P("dp", "ctx", None),
        P("dp", None),
        P("dp", None),
    )
    return jax.shard_map(
        local,
        mesh=mesh,
        in_specs=placed,
        out_specs=(
            P("dp", "ctx", None, "tp"),
            P("dp", "ctx", None, "tp"),
            P("dp", "ctx", None, "tp"),
            P(("ctx", "dp"), "tp"),
        ),
        check_vma=False,
    )
```

```python
import math

import jax
import jax.numpy as jnp
from jax import lax
from jax.experimental import pallas as pl
from jax.experimental.pallas import tpu as pltpu
from jax.sharding import PartitionSpec as P

HD = 128
LOC = 256
BLK = 64
NEG = -1e30
MESH = pl.DeviceIdType.MESH
F32 = jnp.float32
BF16 = jnp.bfloat16
SCALE = HD**-0.5
C2 = SCALE * math.log2(math.e)


def nn(a, b):
    return lax.dot_general(a, b, (((1,), (0,)), ((), ())), preferred_element_type=F32)


def nt(a, b):
    return lax.dot_general(a, b, (((1,), (1,)), ((), ())), preferred_element_type=F32)


def softmax_t(scores, mask):
    s = jnp.where(mask, scores * C2, NEG)
    top = jnp.max(s, axis=0, keepdims=True)
    p = jnp.exp2(s - top)
    return p * (1.0 / jnp.sum(p, axis=0, keepdims=True))


def kernel(
    q_hbm, k_hbm, v_hbm, og_hbm, w_hbm, sdoc_hbm, ldoc_hbm, place_hbm,
    dq_ref, dk_ref, dv_ref, wg_ref,
    q_ref, k_ref, v_ref, sdoc_ref, ldoc_ref, place_ref,
    og_full, og_t, w_full, stage, gstage, hot_in, hot_g, hot_kt, hot_p, hot_at, hot_attn, hot_grads, hot_acc,
    attn_in, grads_in, attn_all, attn_t, p_short, g_acc, g_all, half_out, half_in,
    down_out, down_in, up_out, up_in, red, last_out, last_in,
    in_s, og_s, og_r, w_s, w_r, st_s, gs_s, hin_r, hg_r, ha_s, at_r, ho_s, gr_r,
    half_s, half_r, dn_s, dn_r, up_s, up_r, last_s, last_r,
):
    z = lax.axis_index("ctx")
    dp = lax.axis_index("dp")
    tp = lax.axis_index("tp")
    nz = 16
    y_hi, core = dp // 2, dp % 2
    y_lo, x = tp // 4, tp % 4
    row, other = y_lo * 4, (1 - y_lo) * 4
    xr, xl, xo = (x + 1) % 4, (x + 3) % 4, (x + 2) % 4
    dpo = (1 - y_hi) * 2 + core
    sib = y_hi * 2 + 1 - core
    sibo = (1 - y_hi) * 2 + 1 - core
    right, left = {"tp": row + xr}, {"tp": row + xl}
    pair = {"tp": other + x}
    opposite = {"dp": dpo}
    sibling = {"dp": sib}
    zup, zdn = {"ctx": (z + 1) % nz}, {"ctx": (z + nz - 1) % nz}
    rel = (z + nz - 3 * core) % nz
    is_hot = (rel % 5 == 0) & (rel < 15)
    hot_h = rel // 5

    def rc(src, dst, ss, rs, dev):
        return pltpu.make_async_remote_copy(
            src_ref=src, dst_ref=dst, send_sem=ss, recv_sem=rs, device_id=dev, device_id_type=MESH
        )

    loads = [
        pltpu.make_async_copy(src, dst, in_s.at[i])
        for i, (src, dst) in enumerate(
            (
                (og_hbm, og_full.at[tp]), (k_hbm, k_ref), (q_hbm, q_ref), (v_hbm, v_ref),
                (w_hbm, w_full.at[dp]), (sdoc_hbm, sdoc_ref), (ldoc_hbm, ldoc_ref), (place_hbm, place_ref),
            )
        )
    ]
    for load in loads:
        load.start()

    bar = pltpu.get_barrier_semaphore()
    for dev in (right, left, pair, opposite, sibling):
        pl.semaphore_signal(bar, inc=1, device_id=dev, device_id_type=MESH)

    def greet(i, carry):
        pl.semaphore_signal(bar, inc=1, device_id={"ctx": (z + i) % nz}, device_id_type=MESH)
        return carry

    lax.fori_loop(1, nz, greet, 0)
    for load in loads:
        load.wait()
    pl.semaphore_wait(bar, 20)

    lo, hi = pl.ds(0, 160), pl.ds(160, 160)
    og = [
        (tp, lo, right, row + xl),
        (tp, hi, right, row + xl),
        (other + x, lo, right, other + xl),
        (row + xl, lo, right, row + xo),
        (other + xl, lo, right, other + xo),
        (tp, hi, left, row + xr),
        (tp, lo, left, row + xr),
        (other + x, hi, left, other + xr),
        (row + xr, hi, left, row + xo),
        (other + xr, hi, left, other + xo),
        (tp, lo, pair, other + x),
        (tp, hi, pair, other + x),
        (other + x, hi, right, other + xl),
        (other + x, lo, left, other + xr),
    ]

    def og_copy(i):
        slot, rows, dev, _ = og[i]
        there = og_full.at[slot, rows]
        return rc(there, there, og_s.at[i], og_r.at[i], dev)

    def og_wait(i):
        _, rows, dev, slot = og[i]
        here = og_full.at[slot, rows]
        rc(here, here, og_s.at[i], og_r.at[i], dev).wait_recv()

    def turn(slot):
        t = og_full[slot].astype(F32).T.reshape(4, 2, 40, 320)
        og_t[slot, 0] = t[:, 0].reshape(160, 320).astype(BF16)
        og_t[slot, 1] = t[:, 1].reshape(160, 320).astype(BF16)

    def w_copy(i):
        slot, dev = ((dp, opposite), (dp, sibling), (dpo, sibling))[i]
        there = w_full.at[slot]
        return rc(there, there, w_s.at[i], w_r.at[i], dev)

    def w_wait(i):
        slot = (dpo, sib, sibo)[i]
        here = w_full.at[slot]
        rc(here, here, w_s.at[i], w_r.at[i], sibling).wait_recv()

    for i in (10, 0, 5, 11, 1, 6):
        og_copy(i).start()
    w_copy(0).start()

    def owner(h):
        return 5 * h + 3 * core

    def to_hot(h):
        return rc(stage.at[h], hot_in.at[z], st_s.at[h], hin_r.at[z], {"ctx": owner(h)})

    def g_to_hot(h):
        return rc(gstage.at[h], hot_g.at[z], gs_s.at[h], hg_r.at[z], {"ctx": owner(h)})

    for h in range(3):
        hs = slice(h * HD, (h + 1) * HD)
        stage[h, 0] = q_ref[LOC:, hs]
        stage[h, 1] = k_ref[LOC:, hs]
        stage[h, 2] = v_ref[LOC:, hs]
    for h in range(3):
        @pl.when(z != owner(h))
        def _():
            to_hot(h).start()

        @pl.when(z == owner(h))
        def _():
            hot_in[z] = stage[h]

    w_copy(1).start()

    sid = sdoc_ref[...].astype(F32)
    sid_col = jnp.broadcast_to(sid, (HD, LOC)).T
    sid_col = jnp.concatenate([sid_col, sid_col], axis=1)
    kk = lax.broadcasted_iota(jnp.int32, (LOC, LOC), 0)
    qq = lax.broadcasted_iota(jnp.int32, (LOC, LOC), 1)
    smask = (kk <= qq) & (sid_col == sid)

    def short_forward(h):
        hs = slice(h * HD, (h + 1) * HD)
        p = softmax_t(nt(k_ref[:LOC, hs], q_ref[:LOC, hs]), smask).astype(BF16)
        p_short[h] = p
        at = nn(v_ref[:LOC, hs].T, p).astype(BF16).astype(F32)
        attn_t[h] = at
        attn_all[:LOC, hs] = at.T.astype(BF16)

    short_forward(0)
    short_forward(1)
    og_wait(10)
    og_copy(2).start()
    og_wait(11)
    og_copy(7).start()
    og_wait(0)
    og_copy(3).start()
    og_wait(5)
    og_copy(8).start()
    og_copy(12).start()
    og_copy(13).start()
    og_wait(1)
    og_wait(6)
    short_forward(2)
    turn(tp)
    turn(other + x)
    og_wait(2)
    og_copy(4).start()
    og_wait(7)
    og_copy(9).start()

    def each_other(fn):
        def body(i, carry):
            fn((z + i) % nz)
            return carry

        lax.fori_loop(1, nz, body, 0)

    def attn_back(c):
        return rc(hot_attn.at[c], attn_in.at[hot_h], ha_s.at[c], at_r.at[hot_h], {"ctx": c})

    def grads_back(c):
        return rc(hot_grads.at[c], grads_in.at[hot_h], ho_s.at[c], gr_r.at[hot_h], {"ctx": c})

    @pl.when(is_hot)
    def _():
        each_other(lambda c: rc(hot_in.at[c], hot_in.at[c], st_s.at[0], hin_r.at[c], zup).wait_recv())
        lane = lax.broadcasted_iota(jnp.int32, (1, 1024), 1)
        blk = lane // BLK
        place = jnp.zeros((1, 1024), jnp.int32)
        for c in range(nz):
            place = jnp.where(blk == c, place_ref[0, c], place)
        qpos = place * BLK + lane % BLK
        total = jnp.sum(ldoc_ref[...].astype(F32), axis=1, keepdims=True)
        cut = 1024 - total.astype(jnp.int32)
        qlo = jnp.where(qpos >= cut, cut, 0)
        k_all = hot_in[:, 1].reshape(1024, HD)
        v_t = hot_in[:, 2].reshape(1024, HD).T
        for t in range(4):
            ts = slice(t * 256, (t + 1) * 256)
            q_t = hot_in[4 * t : 4 * t + 4, 0].reshape(256, HD)
            s = nt(k_all, q_t)
            spot = lax.broadcasted_iota(jnp.int32, (BLK, 256), 0)
            kpos = jnp.concatenate([spot + place_ref[0, c] * BLK for c in range(nz)], axis=0)
            mask = (kpos <= qpos[:, ts]) & (kpos >= qlo[:, ts])
            p = softmax_t(s, mask).astype(BF16)
            hot_p[:, ts] = p
            at = nn(v_t, p).astype(BF16).astype(F32)
            hot_at[:, ts] = at
            hot_attn[4 * t : 4 * t + 4] = at.T.astype(BF16).reshape(4, BLK, HD)
            for c in range(4 * t, 4 * t + 4):
                @pl.when(z != c)
                def _():
                    attn_back(c).start()
        hot_kt[...] = k_all.T

    turn(row + xl)
    turn(row + xr)
    og_wait(3)
    og_wait(8)
    turn(row + xo)
    og_wait(12)
    turn(other + xl)
    og_wait(13)
    turn(other + xr)
    og_wait(4)
    og_wait(9)
    turn(other + xo)

    def product(slot, k):
        return nn(og_full[2 * slot + k], w_full[slot, k * 320 : k * 320 + 320])

    w_wait(1)
    g_acc[...] = (product(dp, 0) + product(dp, 1)) + (product(sib, 0) + product(sib, 1))
    w_wait(0)
    w_copy(2).start()
    g_acc[...] += product(dpo, 0) + product(dpo, 1)
    w_wait(2)
    g_all[...] = (g_acc[...] + (product(sibo, 0) + product(sibo, 1))).astype(BF16)
    for h in range(3):
        gstage[h] = g_all[LOC:, h * HD : (h + 1) * HD]
    for h in range(3):
        @pl.when(z != owner(h))
        def _():
            g_to_hot(h).start()

        @pl.when(z == owner(h))
        def _():
            hot_g[z] = gstage[h]

    for h in range(3):
        hs = slice(h * HD, (h + 1) * HD)
        g = g_all[:LOC, hs]
        v, k = v_ref[:LOC, hs], k_ref[:LOC, hs]
        delta = jnp.sum(g.T.astype(F32) * attn_t[h], axis=0, keepdims=True)
        p = p_short[h]
        ds = (p.astype(F32) * (nt(v, g) - delta)).astype(BF16)
        dk_ref[:LOC, hs] = (nn(ds, q_ref[:LOC, hs]) * SCALE).astype(BF16)
        dv_ref[:LOC, hs] = nn(p, g).astype(BF16)
        dq_ref[:LOC, hs] = (nn(k.T, ds).T * SCALE).astype(BF16)

    for h in range(3):
        hs = slice(h * HD, (h + 1) * HD)

        @pl.when(z != owner(h))
        def _():
            rc(attn_in.at[h], attn_in.at[h], gs_s.at[h], at_r.at[h], zup).wait_recv()
            attn_all[LOC:, hs] = attn_in[h]

        @pl.when(z == owner(h))
        def _():
            attn_all[LOC:, hs] = hot_attn[z]

    sign = 1 - 2 * (z % 2)

    def nth(i):
        step = (i + 1) // 2
        return (z // 2 + 12 + (step if i % 2 == 0 else -step) * sign) % 8

    def half(i):
        there = pl.ds(2 * nth(i), 2)
        return rc(half_out.at[there], half_in.at[there], half_s.at[i], half_r.at[i], sibling)

    attn = attn_all[...]
    for i in range(8):
        t = nth(i)
        half_out[pl.ds(2 * t, 2)] = nn(og_t[t, 1 - core], attn).astype(BF16).reshape(2, 80, 384)
        half(i).start()
        red[pl.ds(2 * t, 2)] = nn(og_t[t, core], attn).reshape(2, 80, 384)

    subs = (pl.ds(0, 48), pl.ds(48, 32))

    def down(s, j):
        return rc(down_out.at[s, subs[j]], down_in.at[s, subs[j]], dn_s.at[s, j], dn_r.at[s, j], zdn)

    def up(s, j):
        return rc(up_out.at[s, subs[j]], up_in.at[s, subs[j]], up_s.at[s, j], up_r.at[s, j], zup)

    def mine(c, j):
        return red[c, subs[j]] + half_in[c, subs[j]].astype(F32)

    def ring(s):
        for i in {0: (0, 1), 1: (2, 3), 3: (4, 5), 5: (6, 7)}.get(s, ()):
            half(i).wait_recv()
        for j in range(2):
            v = mine((z + 8 + s) % nz, j)
            if s > 0:
                down(s - 1, j).wait_recv()
                v = v + down_in[s - 1, subs[j]].astype(F32)
            down_out[s, subs[j]] = v.astype(BF16)
            down(s, j).start()
            if s < 7:
                v = mine((z + 7 - s) % nz, j)
                if s > 0:
                    up(s - 1, j).wait_recv()
                    v = v + up_in[s - 1, subs[j]].astype(F32)
                up_out[s, subs[j]] = v.astype(BF16)
                up(s, j).start()

    def hot_back(t):
        ts = slice(t * 256, (t + 1) * 256)
        if t == 0:
            each_other(lambda c: rc(hot_g.at[c], hot_g.at[c], gs_s.at[0], hg_r.at[c], zup).wait_recv())
        g = hot_g[4 * t : 4 * t + 4].reshape(256, HD)
        q = hot_in[4 * t : 4 * t + 4, 0].reshape(256, HD)
        delta = jnp.sum(g.T.astype(F32) * hot_at[:, ts], axis=0, keepdims=True)
        p = hot_p[:, ts]
        ds = (p.astype(F32) * (nt(hot_in[:, 2].reshape(1024, HD), g) - delta)).astype(BF16)
        dk = nn(ds, q)
        dv = nn(p, g)
        if t > 0:
            dk += hot_acc[0]
            dv += hot_acc[1]
        dq = nn(hot_kt[...], ds).T * SCALE
        hot_grads[4 * t : 4 * t + 4, 0] = dq.astype(BF16).reshape(4, BLK, HD)
        if t < 3:
            hot_acc[0] = dk
            hot_acc[1] = dv
        else:
            hot_grads[:, 1] = (dk * SCALE).astype(BF16).reshape(nz, BLK, HD)
            hot_grads[:, 2] = dv.astype(BF16).reshape(nz, BLK, HD)
            each_other(lambda c: grads_back(c).start())

    for s in range(8):
        ring(s)
        if s < 4:
            pl.when(is_hot)(lambda: hot_back(s))
    for j in range(2):
        up(6, j).wait_recv()
        down(7, j).wait_recv()
    total = red[z] + half_in[z].astype(F32) + up_in[6].astype(F32) + down_in[7].astype(F32)
    last_out[...] = total.astype(BF16)
    red[z] = total
    theirs = pl.ds(pl.multiple_of(32 - 32 * y_hi, 16), 48)
    last = rc(last_out.at[theirs], last_in, last_s, last_r, opposite)
    last.start()

    for h in range(3):
        hs = slice(h * HD, (h + 1) * HD)

        @pl.when(z != owner(h))
        def _():
            rc(grads_in.at[h], grads_in.at[h], gs_s.at[h], gr_r.at[h], zup).wait_recv()
            dq_ref[LOC:, hs] = grads_in[h, 0]
            dk_ref[LOC:, hs] = grads_in[h, 1]
            dv_ref[LOC:, hs] = grads_in[h, 2]

        @pl.when(z == owner(h))
        def _():
            dq_ref[LOC:, hs] = hot_grads[z, 0]
            dk_ref[LOC:, hs] = hot_grads[z, 1]
            dv_ref[LOC:, hs] = hot_grads[z, 2]

    for i in range(14):
        og_copy(i).wait_send()
    for i in range(3):
        w_copy(i).wait_send()
    for h in range(3):
        @pl.when(z != owner(h))
        def _():
            to_hot(h).wait_send()
            g_to_hot(h).wait_send()

    @pl.when(is_hot)
    def _():
        each_other(lambda c: attn_back(c).wait_send())
        each_other(lambda c: grads_back(c).wait_send())

    for i in range(8):
        half(i).wait_send()
    for s in range(8):
        for j in range(2):
            down(s, j).wait_send()
            if s < 7:
                up(s, j).wait_send()
    last.wait()
    own = pl.ds(pl.multiple_of(40 * y_hi, 8), 40)
    came = last_in[...].astype(F32)
    wg_ref[...] = red[z, own] + jnp.where(y_hi == 0, came[:40], came[8:])


def local(queries, keys, values, out_grad, out_weight, short_docs, long_docs, block_place):
    vm = pl.BlockSpec(memory_space=pltpu.VMEM)
    hbm = pl.BlockSpec(memory_space=pltpu.HBM)
    dma = pltpu.SemaphoreType.DMA
    dq, dk, dv, wg = pl.pallas_call(
        kernel,
        out_shape=(
            jax.ShapeDtypeStruct((320, 384), BF16),
            jax.ShapeDtypeStruct((320, 384), BF16),
            jax.ShapeDtypeStruct((320, 384), BF16),
            jax.ShapeDtypeStruct((40, 384), F32),
        ),
        in_specs=[hbm] * 8,
        out_specs=(vm,) * 4,
        scratch_shapes=[
            pltpu.VMEM((320, 384), BF16),
            pltpu.VMEM((320, 384), BF16),
            pltpu.VMEM((320, 384), BF16),
            pltpu.VMEM((1, 256), jnp.int32),
            pltpu.VMEM((1, 1024), jnp.int32),
            pltpu.SMEM((1, 16), jnp.int32),
            pltpu.VMEM((8, 320, 320), BF16),
            pltpu.VMEM((8, 2, 160, 320), BF16),
            pltpu.VMEM((4, 640, 384), BF16),
            pltpu.VMEM((3, 3, 64, 128), BF16),
            pltpu.VMEM((3, 64, 128), BF16),
            pltpu.VMEM((16, 3, 64, 128), BF16),
            pltpu.VMEM((16, 64, 128), BF16),
            pltpu.VMEM((128, 1024), BF16),
            pltpu.VMEM((1024, 1024), BF16),
            pltpu.VMEM((128, 1024), F32),
            pltpu.VMEM((16, 64, 128), BF16),
            pltpu.VMEM((16, 3, 64, 128), BF16),
            pltpu.VMEM((2, 1024, 128), F32),
            pltpu.VMEM((3, 64, 128), BF16),
            pltpu.VMEM((3, 3, 64, 128), BF16),
            pltpu.VMEM((320, 384), BF16),
            pltpu.VMEM((3, 128, 256), F32),
            pltpu.VMEM((3, 256, 256), BF16),
            pltpu.VMEM((320, 384), F32),
            pltpu.VMEM((320, 384), BF16),
            pltpu.VMEM((16, 80, 384), BF16),
            pltpu.VMEM((16, 80, 384), BF16),
            pltpu.VMEM((8, 80, 384), BF16),
            pltpu.VMEM((8, 80, 384), BF16),
            pltpu.VMEM((7, 80, 384), BF16),
            pltpu.VMEM((7, 80, 384), BF16),
            pltpu.VMEM((16, 80, 384), F32),
            pltpu.VMEM((80, 384), BF16),
            pltpu.VMEM((48, 384), BF16),
            dma((8,)), dma((14,)), dma((14,)), dma((3,)), dma((3,)),
            dma((3,)), dma((3,)), dma((16,)), dma((16,)),
            dma((16,)), dma((3,)), dma((16,)), dma((3,)),
            dma((8,)), dma((8,)), dma((8, 2)), dma((8, 2)), dma((7, 2)), dma((7, 2)), dma, dma,
        ],
        compiler_params=pltpu.CompilerParams(
            collective_id=0, has_side_effects=True, vmem_limit_bytes=50 * 1024 * 1024
        ),
        name="attention_grads",
    )(
        *(
            pltpu.with_memory_space_constraint(a, pltpu.HBM)
            for a in (
                queries[0, 0], keys[0, 0], values[0, 0], out_grad[0, 0], out_weight,
                short_docs[0], long_docs, block_place,
            )
        )
    )
    shape = queries.shape
    return dq.reshape(shape), dk.reshape(shape), dv.reshape(shape), wg


def solution(mesh):
    placed = (
        P("dp", "ctx", None, "tp"),
        P("dp", "ctx", None, "tp"),
        P("dp", "ctx", None, "tp"),
        P("dp", "ctx", None, "tp"),
        P("dp", "tp"),
        P("dp", "ctx", None),
        P("dp", None),
        P("dp", None),
    )
    return jax.shard_map(
        local,
        mesh=mesh,
        in_specs=placed,
        out_specs=(
            P("dp", "ctx", None, "tp"),
            P("dp", "ctx", None, "tp"),
            P("dp", "ctx", None, "tp"),
            P(("ctx", "dp"), "tp"),
        ),
        check_vma=False,
    )
```

```python
import math

import jax
import jax.numpy as jnp
from jax import lax
from jax.experimental import pallas as pl
from jax.experimental.pallas import tpu as pltpu
from jax.sharding import PartitionSpec as P

HD = 128
LOC = 256
BLK = 64
NEG = -1e30
OWNERS = ((0, 3), (5, 8), (10, 13))
MESH = pl.DeviceIdType.MESH
F32 = jnp.float32
BF16 = jnp.bfloat16
SCALE = HD**-0.5
C2 = SCALE * math.log2(math.e)


def nn(a, b):
    return lax.dot_general(a, b, (((1,), (0,)), ((), ())), preferred_element_type=F32)


def nt(a, b):
    return lax.dot_general(a, b, (((1,), (1,)), ((), ())), preferred_element_type=F32)


def softmax_t(scores, mask):
    s = jnp.where(mask, scores * C2, NEG)
    top = jnp.max(s, axis=0, keepdims=True)
    p = jnp.exp2(s - top)
    return p * (1.0 / jnp.sum(p, axis=0, keepdims=True))


def kernel(
    q_hbm, k_hbm, v_hbm, og_hbm, w_hbm, sdoc_hbm, ldoc_hbm, place_hbm,
    dq_ref, dk_ref, dv_ref, wg_ref,
    q_ref, k_ref, v_ref, sdoc_ref, ldoc_ref, place_ref,
    og_full, og_t, w_full, stage, gstage, hot_in, hot_g, hot_kt, hot_p, hot_at, hot_attn, hot_grads, hot_acc,
    attn_in, grads_in, attn_all, attn_t, p_short, g_acc, g_all, half_out, half_in,
    down_out, down_in, up_out, up_in, red, self_out, fin_in,
    in_s, og_s, og_r, w_s, w_r, st_s, gs_s, hin_r, hg_r, ha_s, at_r, ho_s, gr_r,
    half_s, half_r, dn_s, dn_r, up_s, up_r, fin_s, fin_r,
):
    z = lax.axis_index("ctx")
    dp = lax.axis_index("dp")
    tp = lax.axis_index("tp")
    nz = 16
    y_hi, core = dp // 2, dp % 2
    y_lo, x = tp // 4, tp % 4
    row, other = y_lo * 4, (1 - y_lo) * 4
    xr, xl, xo = (x + 1) % 4, (x + 3) % 4, (x + 2) % 4
    dpo = (1 - y_hi) * 2 + core
    sib = y_hi * 2 + 1 - core
    sibo = (1 - y_hi) * 2 + 1 - core
    right, left = {"tp": row + xr}, {"tp": row + xl}
    pair = {"tp": other + x}
    opposite = {"dp": dpo}
    sibling = {"dp": sib}
    zup, zdn = {"ctx": (z + 1) % nz}, {"ctx": (z + nz - 1) % nz}
    zup_o, zdn_o = {"ctx": (z + 1) % nz, "dp": dpo}, {"ctx": (z + nz - 1) % nz, "dp": dpo}
    owners = [jnp.where(core == 0, a, b) for a, b in OWNERS]
    is_hot = (z == owners[0]) | (z == owners[1]) | (z == owners[2])
    hot_h = jnp.where(z == owners[1], 1, jnp.where(z == owners[2], 2, 0))

    def rc(src, dst, ss, rs, dev):
        return pltpu.make_async_remote_copy(
            src_ref=src, dst_ref=dst, send_sem=ss, recv_sem=rs, device_id=dev, device_id_type=MESH
        )

    loads = [
        pltpu.make_async_copy(src, dst, in_s.at[i])
        for i, (src, dst) in enumerate(
            (
                (og_hbm, og_full.at[tp]), (k_hbm, k_ref), (q_hbm, q_ref), (v_hbm, v_ref),
                (w_hbm, w_full.at[dp]), (sdoc_hbm, sdoc_ref), (ldoc_hbm, ldoc_ref), (place_hbm, place_ref),
            )
        )
    ]
    for load in loads:
        load.start()

    bar = pltpu.get_barrier_semaphore()
    for dev in (right, left, pair, opposite, sibling, zup_o, zdn_o):
        pl.semaphore_signal(bar, inc=1, device_id=dev, device_id_type=MESH)

    def greet(i, carry):
        pl.semaphore_signal(bar, inc=1, device_id={"ctx": (z + i) % nz}, device_id_type=MESH)
        return carry

    for dev in (zup, zdn):
        pl.semaphore_signal(bar, inc=1, device_id=dev, device_id_type=MESH)

    @pl.when(is_hot)
    def _():
        lax.fori_loop(1, nz, greet, 0)

    for load in loads:
        load.wait()
    pl.semaphore_wait(bar, 12 - is_hot.astype(jnp.int32))

    lo, hi = pl.ds(0, 160), pl.ds(160, 160)
    og = [
        (tp, lo, right, row + xl),
        (tp, hi, right, row + xl),
        (other + x, lo, right, other + xl),
        (row + xl, lo, right, row + xo),
        (other + xl, lo, right, other + xo),
        (tp, hi, left, row + xr),
        (tp, lo, left, row + xr),
        (other + x, hi, left, other + xr),
        (row + xr, hi, left, row + xo),
        (other + xr, hi, left, other + xo),
        (tp, lo, pair, other + x),
        (tp, hi, pair, other + x),
        (other + x, hi, right, other + xl),
        (other + x, lo, left, other + xr),
    ]

    def og_copy(i):
        slot, rows, dev, _ = og[i]
        there = og_full.at[slot, rows]
        return rc(there, there, og_s.at[i], og_r.at[i], dev)

    def og_wait(i):
        _, rows, dev, slot = og[i]
        here = og_full.at[slot, rows]
        rc(here, here, og_s.at[i], og_r.at[i], dev).wait_recv()

    def turn(slot):
        t = og_full[slot].astype(F32).T.reshape(4, 2, 40, 320)
        og_t[slot, 0] = t[:, 0].reshape(160, 320).astype(BF16)
        og_t[slot, 1] = t[:, 1].reshape(160, 320).astype(BF16)

    wlo, whi, wall = pl.ds(0, 320), pl.ds(320, 320), pl.ds(0, 640)

    def w_copy(i):
        slot, rows, dev = (
            (dp, wlo, opposite), (dp, whi, opposite), (dp, wall, sibling), (dpo, wlo, sibling), (dpo, whi, sibling),
        )[i]
        there = w_full.at[slot, rows]
        return rc(there, there, w_s.at[i], w_r.at[i], dev)

    def w_wait(i):
        slot, rows = ((dpo, wlo), (dpo, whi), (sib, wall), (sibo, wlo), (sibo, whi))[i]
        here = w_full.at[slot, rows]
        rc(here, here, w_s.at[i], w_r.at[i], sibling).wait_recv()

    for i in (10, 0, 5, 11, 1, 6):
        og_copy(i).start()
    w_copy(0).start()
    w_copy(1).start()

    def owner(h):
        return owners[h]

    parts = (pl.ds(0, 2), pl.ds(2, 1))

    def to_hot(h, n):
        return rc(
            stage.at[h, parts[n]], hot_in.at[z, parts[n]], st_s.at[h, n], hin_r.at[z, n], {"ctx": owner(h)}
        )

    def g_to_hot(h):
        return rc(gstage.at[h], hot_g.at[z], gs_s.at[h], hg_r.at[z], {"ctx": owner(h)})

    for h in range(3):
        hs = slice(h * HD, (h + 1) * HD)
        stage[h, 0] = q_ref[LOC:, hs]
        stage[h, 1] = k_ref[LOC:, hs]
        stage[h, 2] = v_ref[LOC:, hs]
    for n in range(2):
        for h in range(3):
            @pl.when(z != owner(h))
            def _():
                to_hot(h, n).start()

    for h in range(3):
        @pl.when(z == owner(h))
        def _():
            hot_in[z] = stage[h]

    w_copy(2).start()

    sid = sdoc_ref[...].astype(F32)
    sid_col = jnp.broadcast_to(sid, (HD, LOC)).T
    sid_col = jnp.concatenate([sid_col, sid_col], axis=1)
    kk = lax.broadcasted_iota(jnp.int32, (LOC, LOC), 0)
    qq = lax.broadcasted_iota(jnp.int32, (LOC, LOC), 1)
    smask = (kk <= qq) & (sid_col == sid)

    def short_forward(h):
        hs = slice(h * HD, (h + 1) * HD)
        p = softmax_t(nt(k_ref[:LOC, hs], q_ref[:LOC, hs]), smask).astype(BF16)
        p_short[h] = p
        at = nn(v_ref[:LOC, hs].T, p).astype(BF16).astype(F32)
        attn_t[h] = at
        attn_all[:LOC, hs] = at.T.astype(BF16)

    short_forward(0)
    short_forward(1)
    og_wait(10)
    og_copy(2).start()
    og_wait(11)
    og_copy(7).start()
    og_wait(0)
    og_copy(3).start()
    og_wait(5)
    og_copy(8).start()
    og_copy(12).start()
    og_copy(13).start()
    og_wait(1)
    og_wait(6)
    short_forward(2)
    turn(tp)
    turn(other + x)
    og_wait(2)
    og_copy(4).start()
    og_wait(7)
    og_copy(9).start()

    def each_other(fn):
        def body(i, carry):
            fn((z + i) % nz)
            return carry

        lax.fori_loop(1, nz, body, 0)

    def attn_back(c):
        return rc(hot_attn.at[c], attn_in.at[hot_h], ha_s.at[c], at_r.at[hot_h], {"ctx": c})

    def dq_back(c):
        part = pl.ds(0, 1)
        return rc(hot_grads.at[c, part], grads_in.at[hot_h, part], ho_s.at[0, c], gr_r.at[0, hot_h], {"ctx": c})

    def dkv_back(c):
        part = pl.ds(1, 2)
        return rc(hot_grads.at[c, part], grads_in.at[hot_h, part], ho_s.at[1, c], gr_r.at[1, hot_h], {"ctx": c})

    @pl.when(is_hot)
    def _():
        def hot_wait(n):
            each_other(
                lambda c: rc(
                    hot_in.at[c, parts[n]], hot_in.at[c, parts[n]], st_s.at[0, n], hin_r.at[c, n], zup
                ).wait_recv()
            )

        hot_wait(0)
        lane = lax.broadcasted_iota(jnp.int32, (1, 1024), 1)
        blk = lane // BLK
        place = jnp.zeros((1, 1024), jnp.int32)
        for c in range(nz):
            place = jnp.where(blk == c, place_ref[0, c], place)
        qpos = place * BLK + lane % BLK
        total = jnp.sum(ldoc_ref[...].astype(F32), axis=1, keepdims=True)
        cut = 1024 - total.astype(jnp.int32)
        qlo = jnp.where(qpos >= cut, cut, 0)
        k_all = hot_in[:, 1].reshape(1024, HD)
        spot = lax.broadcasted_iota(jnp.int32, (BLK, 256), 0)
        kpos = jnp.concatenate([spot + place_ref[0, c] * BLK for c in range(nz)], axis=0)

        def weigh(t):
            ts = slice(t * 256, (t + 1) * 256)
            q_t = hot_in[4 * t : 4 * t + 4, 0].reshape(256, HD)
            mask = (kpos <= qpos[:, ts]) & (kpos >= qlo[:, ts])
            hot_p[:, ts] = softmax_t(nt(k_all, q_t), mask).astype(BF16)

        weigh(0)
        weigh(1)
        hot_wait(1)
        v_t = hot_in[:, 2].reshape(1024, HD).T
        for t in range(4):
            ts = slice(t * 256, (t + 1) * 256)
            if t > 1:
                weigh(t)
            at = nn(v_t, hot_p[:, ts]).astype(BF16).astype(F32)
            hot_at[:, ts] = at
            hot_attn[4 * t : 4 * t + 4] = at.T.astype(BF16).reshape(4, BLK, HD)
            for c in range(4 * t, 4 * t + 4):
                @pl.when(z != c)
                def _():
                    attn_back(c).start()
        hot_kt[...] = k_all.T

    turn(row + xl)
    turn(row + xr)
    og_wait(3)
    og_wait(8)
    turn(row + xo)
    og_wait(12)
    turn(other + xl)
    og_wait(13)
    turn(other + xr)
    og_wait(4)
    og_wait(9)
    turn(other + xo)

    def product(slot, k):
        return nn(og_full[2 * slot + k], w_full[slot, k * 320 : k * 320 + 320])

    w_wait(2)
    g_acc[...] = (product(dp, 0) + product(dp, 1)) + (product(sib, 0) + product(sib, 1))
    w_wait(0)
    w_copy(3).start()
    w_wait(1)
    w_copy(4).start()
    g_acc[...] += product(dpo, 0) + product(dpo, 1)
    w_wait(3)
    w_wait(4)
    g_all[...] = (g_acc[...] + (product(sibo, 0) + product(sibo, 1))).astype(BF16)
    for h in range(3):
        gstage[h] = g_all[LOC:, h * HD : (h + 1) * HD]
    for h in range(3):
        @pl.when(z != owner(h))
        def _():
            g_to_hot(h).start()

        @pl.when(z == owner(h))
        def _():
            hot_g[z] = gstage[h]

    for h in range(3):
        hs = slice(h * HD, (h + 1) * HD)
        g = g_all[:LOC, hs]
        v, k = v_ref[:LOC, hs], k_ref[:LOC, hs]
        delta = jnp.sum(g.T.astype(F32) * attn_t[h], axis=0, keepdims=True)
        p = p_short[h]
        ds = (p.astype(F32) * (nt(v, g) - delta)).astype(BF16)
        dk_ref[:LOC, hs] = (nn(ds, q_ref[:LOC, hs]) * SCALE).astype(BF16)
        dv_ref[:LOC, hs] = nn(p, g).astype(BF16)
        dq_ref[:LOC, hs] = (nn(k.T, ds).T * SCALE).astype(BF16)

    for h in range(3):
        hs = slice(h * HD, (h + 1) * HD)

        @pl.when(z != owner(h))
        def _():
            rc(attn_in.at[h], attn_in.at[h], gs_s.at[h], at_r.at[h], zup).wait_recv()
            attn_all[LOC:, hs] = attn_in[h]

        @pl.when(z == owner(h))
        def _():
            attn_all[LOC:, hs] = hot_attn[z]

    sign = 1 - 2 * (z % 2)

    def nth(i):
        step = (i + 1) // 2
        return (z // 2 + 12 + (step if i % 2 == 0 else -step) * sign) % 8

    def half(i):
        there = pl.ds(2 * nth(i), 2)
        return rc(half_out.at[there], half_in.at[there], half_s.at[i], half_r.at[i], sibling)

    attn = attn_all[...]
    for i in range(8):
        t = nth(i)
        half_out[pl.ds(2 * t, 2)] = nn(og_t[t, 1 - core], attn).astype(BF16).reshape(2, 80, 384)
        half(i).start()
        red[pl.ds(2 * t, 2)] = nn(og_t[t, core], attn).reshape(2, 80, 384)

    subs = (pl.ds(0, 48), pl.ds(48, 32))

    def down(s, j):
        return rc(down_out.at[s, subs[j]], down_in.at[s, subs[j]], dn_s.at[s, j], dn_r.at[s, j], zdn)

    def up(s, j):
        return rc(up_out.at[s, subs[j]], up_in.at[s, subs[j]], up_s.at[s, j], up_r.at[s, j], zup)

    def mine(c, j):
        return red[c, subs[j]] + half_in[c, subs[j]].astype(F32)

    def ring(s):
        for i in {0: (0, 1), 1: (2, 3), 3: (4, 5), 5: (6, 7)}.get(s, ()):
            half(i).wait_recv()
        for j in range(2):
            v = mine((z + 8 + s) % nz, j)
            if s > 0:
                down(s - 1, j).wait_recv()
                v = v + down_in[s - 1, subs[j]].astype(F32)
            down_out[s, subs[j]] = v.astype(BF16)
            if s < 7:
                down(s, j).start()
                v = mine((z + 7 - s) % nz, j)
                if s > 0:
                    up(s - 1, j).wait_recv()
                    v = v + up_in[s - 1, subs[j]].astype(F32)
                up_out[s, subs[j]] = v.astype(BF16)
                if s < 6:
                    up(s, j).start()
        if s == 5:
            self_out[...] = (red[z] + half_in[z].astype(F32)).astype(BF16)
            final(4).start()
        if s == 6:
            final(2).start()
            final(3).start()
        if s == 7:
            final(0).start()
            final(1).start()

    ours, theirs = (pl.ds(pl.multiple_of(32 * k, 16), 48) for k in (y_hi, 1 - y_hi))

    def final(i):
        src, rows, dev = (
            (down_out.at[7], ours, zdn), (down_out.at[7], theirs, zdn_o),
            (up_out.at[6], ours, zup), (up_out.at[6], theirs, zup_o), (self_out, theirs, opposite),
        )[i]
        return rc(src.at[rows], fin_in.at[i], fin_s.at[i], fin_r.at[i], dev)

    def hot_back(t):
        ts = slice(t * 256, (t + 1) * 256)
        if t == 0:
            each_other(lambda c: rc(hot_g.at[c], hot_g.at[c], gs_s.at[0], hg_r.at[c], zup).wait_recv())
        g = hot_g[4 * t : 4 * t + 4].reshape(256, HD)
        q = hot_in[4 * t : 4 * t + 4, 0].reshape(256, HD)
        delta = jnp.sum(g.T.astype(F32) * hot_at[:, ts], axis=0, keepdims=True)
        p = hot_p[:, ts]
        ds = (p.astype(F32) * (nt(hot_in[:, 2].reshape(1024, HD), g) - delta)).astype(BF16)
        dk = nn(ds, q)
        dv = nn(p, g)
        if t > 0:
            dk += hot_acc[0]
            dv += hot_acc[1]
        dq = nn(hot_kt[...], ds).T * SCALE
        hot_grads[4 * t : 4 * t + 4, 0] = dq.astype(BF16).reshape(4, BLK, HD)
        for c in range(4 * t, 4 * t + 4):
            @pl.when(z != c)
            def _():
                dq_back(c).start()
        if t < 3:
            hot_acc[0] = dk
            hot_acc[1] = dv
        else:
            hot_grads[:, 1] = (dk * SCALE).astype(BF16).reshape(nz, BLK, HD)
            hot_grads[:, 2] = dv.astype(BF16).reshape(nz, BLK, HD)
            each_other(lambda c: dkv_back(c).start())

    for s in range(8):
        ring(s)
        if 2 <= s <= 5:
            pl.when(is_hot)(lambda: hot_back(s - 2))
    for h in range(3):
        hs = slice(h * HD, (h + 1) * HD)

        @pl.when(z != owner(h))
        def _():
            for n, part in enumerate((pl.ds(0, 1), pl.ds(1, 2))):
                rc(grads_in.at[h, part], grads_in.at[h, part], gs_s.at[h], gr_r.at[n, h], zup).wait_recv()
            dq_ref[LOC:, hs] = grads_in[h, 0]
            dk_ref[LOC:, hs] = grads_in[h, 1]
            dv_ref[LOC:, hs] = grads_in[h, 2]

        @pl.when(z == owner(h))
        def _():
            dq_ref[LOC:, hs] = hot_grads[z, 0]
            dk_ref[LOC:, hs] = hot_grads[z, 1]
            dv_ref[LOC:, hs] = hot_grads[z, 2]

    for i in range(14):
        og_copy(i).wait_send()
    for i in range(5):
        w_copy(i).wait_send()
    for h in range(3):
        @pl.when(z != owner(h))
        def _():
            to_hot(h, 0).wait_send()
            to_hot(h, 1).wait_send()
            g_to_hot(h).wait_send()

    @pl.when(is_hot)
    def _():
        each_other(lambda c: attn_back(c).wait_send())
        each_other(lambda c: dq_back(c).wait_send())
        each_other(lambda c: dkv_back(c).wait_send())

    for i in range(8):
        half(i).wait_send()
    for s in range(8):
        for j in range(2):
            if s < 7:
                down(s, j).wait_send()
            if s < 6:
                up(s, j).wait_send()
    for i in range(5):
        final(i).wait()
    total = red[z] + half_in[z].astype(F32)
    low, high = total[:40], total[40:]
    for i in range(5):
        came = fin_in[i].astype(F32)
        low, high = low + came[:40], high + came[8:]
    wg_ref[...] = jnp.where(y_hi == 0, low, high)


def local(queries, keys, values, out_grad, out_weight, short_docs, long_docs, block_place):
    vm = pl.BlockSpec(memory_space=pltpu.VMEM)
    hbm = pl.BlockSpec(memory_space=pltpu.HBM)
    dma = pltpu.SemaphoreType.DMA
    dq, dk, dv, wg = pl.pallas_call(
        kernel,
        out_shape=(
            jax.ShapeDtypeStruct((320, 384), BF16),
            jax.ShapeDtypeStruct((320, 384), BF16),
            jax.ShapeDtypeStruct((320, 384), BF16),
            jax.ShapeDtypeStruct((40, 384), F32),
        ),
        in_specs=[hbm] * 8,
        out_specs=(vm,) * 4,
        scratch_shapes=[
            pltpu.VMEM((320, 384), BF16),
            pltpu.VMEM((320, 384), BF16),
            pltpu.VMEM((320, 384), BF16),
            pltpu.VMEM((1, 256), jnp.int32),
            pltpu.VMEM((1, 1024), jnp.int32),
            pltpu.SMEM((1, 16), jnp.int32),
            pltpu.VMEM((8, 320, 320), BF16),
            pltpu.VMEM((8, 2, 160, 320), BF16),
            pltpu.VMEM((4, 640, 384), BF16),
            pltpu.VMEM((3, 3, 64, 128), BF16),
            pltpu.VMEM((3, 64, 128), BF16),
            pltpu.VMEM((16, 3, 64, 128), BF16),
            pltpu.VMEM((16, 64, 128), BF16),
            pltpu.VMEM((128, 1024), BF16),
            pltpu.VMEM((1024, 1024), BF16),
            pltpu.VMEM((128, 1024), F32),
            pltpu.VMEM((16, 64, 128), BF16),
            pltpu.VMEM((16, 3, 64, 128), BF16),
            pltpu.VMEM((2, 1024, 128), F32),
            pltpu.VMEM((3, 64, 128), BF16),
            pltpu.VMEM((3, 3, 64, 128), BF16),
            pltpu.VMEM((320, 384), BF16),
            pltpu.VMEM((3, 128, 256), F32),
            pltpu.VMEM((3, 256, 256), BF16),
            pltpu.VMEM((320, 384), F32),
            pltpu.VMEM((320, 384), BF16),
            pltpu.VMEM((16, 80, 384), BF16),
            pltpu.VMEM((16, 80, 384), BF16),
            pltpu.VMEM((8, 80, 384), BF16),
            pltpu.VMEM((8, 80, 384), BF16),
            pltpu.VMEM((7, 80, 384), BF16),
            pltpu.VMEM((7, 80, 384), BF16),
            pltpu.VMEM((16, 80, 384), F32),
            pltpu.VMEM((80, 384), BF16),
            pltpu.VMEM((5, 48, 384), BF16),
            dma((8,)), dma((14,)), dma((14,)), dma((5,)), dma((5,)),
            dma((3, 2)), dma((3,)), dma((16, 2)), dma((16,)),
            dma((16,)), dma((3,)), dma((2, 16)), dma((2, 3)),
            dma((8,)), dma((8,)), dma((8, 2)), dma((8, 2)), dma((7, 2)), dma((7, 2)), dma((5,)), dma((5,)),
        ],
        compiler_params=pltpu.CompilerParams(
            collective_id=0, has_side_effects=True, vmem_limit_bytes=50 * 1024 * 1024
        ),
        name="attention_grads",
    )(
        *(
            pltpu.with_memory_space_constraint(a, pltpu.HBM)
            for a in (
                queries[0, 0], keys[0, 0], values[0, 0], out_grad[0, 0], out_weight,
                short_docs[0], long_docs, block_place,
            )
        )
    )
    shape = queries.shape
    return dq.reshape(shape), dk.reshape(shape), dv.reshape(shape), wg


def solution(mesh):
    placed = (
        P("dp", "ctx", None, "tp"),
        P("dp", "ctx", None, "tp"),
        P("dp", "ctx", None, "tp"),
        P("dp", "ctx", None, "tp"),
        P("dp", "tp"),
        P("dp", "ctx", None),
        P("dp", None),
        P("dp", None),
    )
    return jax.shard_map(
        local,
        mesh=mesh,
        in_specs=placed,
        out_specs=(
            P("dp", "ctx", None, "tp"),
            P("dp", "ctx", None, "tp"),
            P("dp", "ctx", None, "tp"),
            P(("ctx", "dp"), "tp"),
        ),
        check_vma=False,
    )
```

```python
import math

import jax
import jax.numpy as jnp
from jax import lax
from jax.experimental import pallas as pl
from jax.experimental.pallas import tpu as pltpu
from jax.sharding import PartitionSpec as P

HD = 128
LOC = 256
BLK = 64
NEG = -1e30
OWNERS = ((0, 3), (6, 8), (11, 14))
MESH = pl.DeviceIdType.MESH
F32 = jnp.float32
BF16 = jnp.bfloat16
SCALE = HD**-0.5
C2 = SCALE * math.log2(math.e)


def nn(a, b):
    return lax.dot_general(a, b, (((1,), (0,)), ((), ())), preferred_element_type=F32)


def nt(a, b):
    return lax.dot_general(a, b, (((1,), (1,)), ((), ())), preferred_element_type=F32)


def softmax_t(scores, mask):
    s = jnp.where(mask, scores * C2, NEG)
    top = jnp.max(s, axis=0, keepdims=True)
    p = jnp.exp2(s - top)
    return p * (1.0 / jnp.sum(p, axis=0, keepdims=True))


def kernel(
    q_hbm, k_hbm, v_hbm, og_hbm, w_hbm, sdoc_hbm, ldoc_hbm, place_hbm,
    dq_ref, dk_ref, dv_ref, wg_ref,
    q_ref, k_ref, v_ref, sdoc_ref, ldoc_ref, place_ref,
    og_full, og_t, w_full, stage, gstage, hot_in, hot_g, hot_kt, hot_p, hot_at, hot_attn, hot_grads, hot_acc,
    attn_in, grads_in, attn_all, attn_t, p_short, g_acc, g_all, half_out, half_in,
    down_out, down_in, up_out, up_in, red, self_out, fin_in,
    in_s, og_s, og_r, w_s, w_r, st_s, gs_s, hin_r, hg_r, ha_s, at_r, ho_s, gr_r,
    half_s, half_r, dn_s, dn_r, up_s, up_r, fin_s, fin_r,
):
    z = lax.axis_index("ctx")
    dp = lax.axis_index("dp")
    tp = lax.axis_index("tp")
    nz = 16
    y_hi, core = dp // 2, dp % 2
    y_lo, x = tp // 4, tp % 4
    row, other = y_lo * 4, (1 - y_lo) * 4
    xr, xl, xo = (x + 1) % 4, (x + 3) % 4, (x + 2) % 4
    dpo = (1 - y_hi) * 2 + core
    sib = y_hi * 2 + 1 - core
    sibo = (1 - y_hi) * 2 + 1 - core
    right, left = {"tp": row + xr}, {"tp": row + xl}
    pair = {"tp": other + x}
    opposite = {"dp": dpo}
    sibling = {"dp": sib}
    zup, zdn = {"ctx": (z + 1) % nz}, {"ctx": (z + nz - 1) % nz}
    zup_o, zdn_o = {"ctx": (z + 1) % nz, "dp": dpo}, {"ctx": (z + nz - 1) % nz, "dp": dpo}
    owners = [jnp.where(core == 0, a, b) for a, b in OWNERS]
    is_hot = (z == owners[0]) | (z == owners[1]) | (z == owners[2])
    hot_h = jnp.where(z == owners[1], 1, jnp.where(z == owners[2], 2, 0))

    def rc(src, dst, ss, rs, dev):
        return pltpu.make_async_remote_copy(
            src_ref=src, dst_ref=dst, send_sem=ss, recv_sem=rs, device_id=dev, device_id_type=MESH
        )

    loads = [
        pltpu.make_async_copy(src, dst, in_s.at[i])
        for i, (src, dst) in enumerate(
            (
                (og_hbm, og_full.at[tp]), (k_hbm, k_ref), (q_hbm, q_ref), (v_hbm, v_ref),
                (w_hbm, w_full.at[dp]), (sdoc_hbm, sdoc_ref), (ldoc_hbm, ldoc_ref), (place_hbm, place_ref),
            )
        )
    ]
    for load in loads:
        load.start()

    bar = pltpu.get_barrier_semaphore()
    for dev in (right, left, pair, opposite, sibling, zup_o, zdn_o):
        pl.semaphore_signal(bar, inc=1, device_id=dev, device_id_type=MESH)

    def greet(i, carry):
        pl.semaphore_signal(bar, inc=1, device_id={"ctx": (z + i) % nz}, device_id_type=MESH)
        return carry

    for dev in (zup, zdn):
        pl.semaphore_signal(bar, inc=1, device_id=dev, device_id_type=MESH)

    @pl.when(is_hot)
    def _():
        lax.fori_loop(1, nz, greet, 0)

    for load in loads:
        load.wait()
    pl.semaphore_wait(bar, 12 - is_hot.astype(jnp.int32))

    lo, hi = pl.ds(0, 160), pl.ds(160, 160)
    og = [
        (tp, lo, right, row + xl),
        (tp, hi, right, row + xl),
        (other + x, lo, right, other + xl),
        (row + xl, lo, right, row + xo),
        (other + xl, lo, right, other + xo),
        (tp, hi, left, row + xr),
        (tp, lo, left, row + xr),
        (other + x, hi, left, other + xr),
        (row + xr, hi, left, row + xo),
        (other + xr, hi, left, other + xo),
        (tp, lo, pair, other + x),
        (tp, hi, pair, other + x),
        (other + x, hi, right, other + xl),
        (other + x, lo, left, other + xr),
    ]

    def og_copy(i):
        slot, rows, dev, _ = og[i]
        there = og_full.at[slot, rows]
        return rc(there, there, og_s.at[i], og_r.at[i], dev)

    def og_wait(i):
        _, rows, dev, slot = og[i]
        here = og_full.at[slot, rows]
        rc(here, here, og_s.at[i], og_r.at[i], dev).wait_recv()

    def turn(slot):
        t = og_full[slot].astype(F32).T.reshape(4, 2, 40, 320)
        og_t[slot, 0] = t[:, 0].reshape(160, 320).astype(BF16)
        og_t[slot, 1] = t[:, 1].reshape(160, 320).astype(BF16)

    wlo, whi, wall = pl.ds(0, 320), pl.ds(320, 320), pl.ds(0, 640)

    def w_copy(i):
        slot, rows, dev = (
            (dp, wlo, opposite), (dp, whi, opposite), (dp, wall, sibling), (dpo, wlo, sibling), (dpo, whi, sibling),
        )[i]
        there = w_full.at[slot, rows]
        return rc(there, there, w_s.at[i], w_r.at[i], dev)

    def w_wait(i):
        slot, rows = ((dpo, wlo), (dpo, whi), (sib, wall), (sibo, wlo), (sibo, whi))[i]
        here = w_full.at[slot, rows]
        rc(here, here, w_s.at[i], w_r.at[i], sibling).wait_recv()

    for i in (10, 0, 5, 11, 1, 6):
        og_copy(i).start()
    w_copy(0).start()
    w_copy(1).start()

    def owner(h):
        return owners[h]

    parts = (pl.ds(0, 2), pl.ds(2, 1))

    def to_hot(h, n):
        return rc(
            stage.at[h, parts[n]], hot_in.at[z, parts[n]], st_s.at[h, n], hin_r.at[z, n], {"ctx": owner(h)}
        )

    def g_to_hot(h):
        return rc(gstage.at[h], hot_g.at[z], gs_s.at[h], hg_r.at[z], {"ctx": owner(h)})

    for h in range(3):
        hs = slice(h * HD, (h + 1) * HD)
        stage[h, 0] = q_ref[LOC:, hs]
        stage[h, 1] = k_ref[LOC:, hs]
        stage[h, 2] = v_ref[LOC:, hs]
    for n in range(2):
        for h in range(3):
            @pl.when(z != owner(h))
            def _():
                to_hot(h, n).start()

    for h in range(3):
        @pl.when(z == owner(h))
        def _():
            hot_in[z] = stage[h]

    w_copy(2).start()

    sid = sdoc_ref[...].astype(F32)
    sid_col = jnp.broadcast_to(sid, (HD, LOC)).T
    sid_col = jnp.concatenate([sid_col, sid_col], axis=1)
    kk = lax.broadcasted_iota(jnp.int32, (LOC, LOC), 0)
    qq = lax.broadcasted_iota(jnp.int32, (LOC, LOC), 1)
    smask = (kk <= qq) & (sid_col == sid)

    def short_forward(h):
        hs = slice(h * HD, (h + 1) * HD)
        p = softmax_t(nt(k_ref[:LOC, hs], q_ref[:LOC, hs]), smask).astype(BF16)
        p_short[h] = p
        at = nn(v_ref[:LOC, hs].T, p).astype(BF16).astype(F32)
        attn_t[h] = at
        attn_all[:LOC, hs] = at.T.astype(BF16)

    short_forward(0)
    short_forward(1)
    og_wait(10)
    og_copy(2).start()
    og_wait(11)
    og_copy(7).start()
    og_wait(0)
    og_copy(3).start()
    og_wait(5)
    og_copy(8).start()
    og_copy(12).start()
    og_copy(13).start()
    og_wait(1)
    og_wait(6)
    short_forward(2)
    turn(tp)
    turn(other + x)
    og_wait(2)
    og_copy(4).start()
    og_wait(7)
    og_copy(9).start()

    def each_other(fn):
        def body(i, carry):
            fn((z + i) % nz)
            return carry

        lax.fori_loop(1, nz, body, 0)

    def attn_back(c):
        return rc(hot_attn.at[c], attn_in.at[hot_h], ha_s.at[c], at_r.at[hot_h], {"ctx": c})

    def dq_back(c):
        part = pl.ds(0, 1)
        return rc(hot_grads.at[c, part], grads_in.at[hot_h, part], ho_s.at[0, c], gr_r.at[0, hot_h], {"ctx": c})

    def dkv_back(c):
        part = pl.ds(1, 2)
        return rc(hot_grads.at[c, part], grads_in.at[hot_h, part], ho_s.at[1, c], gr_r.at[1, hot_h], {"ctx": c})

    @pl.when(is_hot)
    def _():
        def hot_wait(n):
            each_other(
                lambda c: rc(
                    hot_in.at[c, parts[n]], hot_in.at[c, parts[n]], st_s.at[0, n], hin_r.at[c, n], zup
                ).wait_recv()
            )

        hot_wait(0)
        lane = lax.broadcasted_iota(jnp.int32, (1, 1024), 1)
        blk = lane // BLK
        place = jnp.zeros((1, 1024), jnp.int32)
        for c in range(nz):
            place = jnp.where(blk == c, place_ref[0, c], place)
        qpos = place * BLK + lane % BLK
        total = jnp.sum(ldoc_ref[...].astype(F32), axis=1, keepdims=True)
        cut = 1024 - total.astype(jnp.int32)
        qlo = jnp.where(qpos >= cut, cut, 0)
        k_all = hot_in[:, 1].reshape(1024, HD)
        spot = lax.broadcasted_iota(jnp.int32, (BLK, 256), 0)
        kpos = jnp.concatenate([spot + place_ref[0, c] * BLK for c in range(nz)], axis=0)

        def weigh(t):
            ts = slice(t * 256, (t + 1) * 256)
            q_t = hot_in[4 * t : 4 * t + 4, 0].reshape(256, HD)
            mask = (kpos <= qpos[:, ts]) & (kpos >= qlo[:, ts])
            hot_p[:, ts] = softmax_t(nt(k_all, q_t), mask).astype(BF16)

        weigh(0)
        weigh(1)
        hot_wait(1)
        v_t = hot_in[:, 2].reshape(1024, HD).T
        for t in range(4):
            ts = slice(t * 256, (t + 1) * 256)
            if t > 1:
                weigh(t)
            at = nn(v_t, hot_p[:, ts]).astype(BF16).astype(F32)
            hot_at[:, ts] = at
            hot_attn[4 * t : 4 * t + 4] = at.T.astype(BF16).reshape(4, BLK, HD)
            for c in range(4 * t, 4 * t + 4):
                @pl.when(z != c)
                def _():
                    attn_back(c).start()
        hot_kt[...] = k_all.T

    turn(row + xl)
    turn(row + xr)
    og_wait(3)
    og_wait(8)
    turn(row + xo)
    og_wait(12)
    turn(other + xl)
    og_wait(13)
    turn(other + xr)
    og_wait(4)
    og_wait(9)
    turn(other + xo)

    def product(slot, k):
        return nn(og_full[2 * slot + k], w_full[slot, k * 320 : k * 320 + 320])

    w_wait(2)
    g_acc[...] = (product(dp, 0) + product(dp, 1)) + (product(sib, 0) + product(sib, 1))
    w_wait(0)
    w_copy(3).start()
    w_wait(1)
    w_copy(4).start()
    g_acc[...] += product(dpo, 0) + product(dpo, 1)
    w_wait(3)
    w_wait(4)
    g_all[...] = (g_acc[...] + (product(sibo, 0) + product(sibo, 1))).astype(BF16)
    for h in range(3):
        gstage[h] = g_all[LOC:, h * HD : (h + 1) * HD]
    for h in range(3):
        @pl.when(z != owner(h))
        def _():
            g_to_hot(h).start()

        @pl.when(z == owner(h))
        def _():
            hot_g[z] = gstage[h]

    for h in range(3):
        hs = slice(h * HD, (h + 1) * HD)

        @pl.when(z != owner(h))
        def _():
            rc(attn_in.at[h], attn_in.at[h], gs_s.at[h], at_r.at[h], zup).wait_recv()
            attn_all[LOC:, hs] = attn_in[h]

        @pl.when(z == owner(h))
        def _():
            attn_all[LOC:, hs] = hot_attn[z]

    sign = 1 - 2 * (z % 2)

    def nth(i):
        step = (i + 1) // 2
        return (z // 2 + 12 + (step if i % 2 == 0 else -step) * sign) % 8

    def half(i):
        there = pl.ds(2 * nth(i), 2)
        return rc(half_out.at[there], half_in.at[there], half_s.at[i], half_r.at[i], sibling)

    def piece(i):
        t = nth(i)
        attn = attn_all[...]
        half_out[pl.ds(2 * t, 2)] = nn(og_t[t, 1 - core], attn).astype(BF16).reshape(2, 80, 384)
        half(i).start()
        red[pl.ds(2 * t, 2)] = nn(og_t[t, core], attn).reshape(2, 80, 384)

    for i in range(4):
        piece(i)

    subs = (pl.ds(0, 32), pl.ds(32, 32), pl.ds(64, 16))

    def down(s, j):
        return rc(down_out.at[s, subs[j]], down_in.at[s, subs[j]], dn_s.at[s, j], dn_r.at[s, j], zdn)

    def up(s, j):
        return rc(up_out.at[s, subs[j]], up_in.at[s, subs[j]], up_s.at[s, j], up_r.at[s, j], zup)

    def mine(c, j):
        return red[c, subs[j]] + half_in[c, subs[j]].astype(F32)

    def ring(s):
        for i in {0: (0, 1), 1: (2, 3), 3: (4, 5), 5: (6, 7)}.get(s, ()):
            half(i).wait_recv()
        for j in range(3):
            v = mine((z + 8 + s) % nz, j)
            if s > 0:
                down(s - 1, j).wait_recv()
                v = v + down_in[s - 1, subs[j]].astype(F32)
            down_out[s, subs[j]] = v.astype(BF16)
            if s < 7:
                down(s, j).start()
                v = mine((z + 7 - s) % nz, j)
                if s > 0:
                    up(s - 1, j).wait_recv()
                    v = v + up_in[s - 1, subs[j]].astype(F32)
                up_out[s, subs[j]] = v.astype(BF16)
                if s < 6:
                    up(s, j).start()
        if s == 5:
            self_out[...] = (red[z] + half_in[z].astype(F32)).astype(BF16)
            final(4).start()
        if s == 6:
            final(2).start()
            final(3).start()
        if s == 7:
            final(0).start()
            final(1).start()

    ours, theirs = (pl.ds(pl.multiple_of(32 * k, 16), 48) for k in (y_hi, 1 - y_hi))

    def final(i):
        src, rows, dev = (
            (down_out.at[7], ours, zdn), (down_out.at[7], theirs, zdn_o),
            (up_out.at[6], ours, zup), (up_out.at[6], theirs, zup_o), (self_out, theirs, opposite),
        )[i]
        return rc(src.at[rows], fin_in.at[i], fin_s.at[i], fin_r.at[i], dev)

    def hot_back(t):
        ts = slice(t * 256, (t + 1) * 256)
        if t == 0:
            each_other(lambda c: rc(hot_g.at[c], hot_g.at[c], gs_s.at[0], hg_r.at[c], zup).wait_recv())
        g = hot_g[4 * t : 4 * t + 4].reshape(256, HD)
        q = hot_in[4 * t : 4 * t + 4, 0].reshape(256, HD)
        delta = jnp.sum(g.T.astype(F32) * hot_at[:, ts], axis=0, keepdims=True)
        p = hot_p[:, ts]
        ds = (p.astype(F32) * (nt(hot_in[:, 2].reshape(1024, HD), g) - delta)).astype(BF16)
        dk = nn(ds, q)
        dv = nn(p, g)
        if t > 0:
            dk += hot_acc[0]
            dv += hot_acc[1]
        dq = nn(hot_kt[...], ds).T * SCALE
        hot_grads[4 * t : 4 * t + 4, 0] = dq.astype(BF16).reshape(4, BLK, HD)
        for c in range(4 * t, 4 * t + 4):
            @pl.when(z != c)
            def _():
                dq_back(c).start()
        if t < 3:
            hot_acc[0] = dk
            hot_acc[1] = dv
        else:
            hot_grads[:, 1] = (dk * SCALE).astype(BF16).reshape(nz, BLK, HD)
            hot_grads[:, 2] = dv.astype(BF16).reshape(nz, BLK, HD)
            each_other(lambda c: dkv_back(c).start())

    ring(0)
    for i in range(4, 8):
        piece(i)

    for h in range(3):
        hs = slice(h * HD, (h + 1) * HD)
        g = g_all[:LOC, hs]
        v, k = v_ref[:LOC, hs], k_ref[:LOC, hs]
        delta = jnp.sum(g.T.astype(F32) * attn_t[h], axis=0, keepdims=True)
        p = p_short[h]
        ds = (p.astype(F32) * (nt(v, g) - delta)).astype(BF16)
        dk_ref[:LOC, hs] = (nn(ds, q_ref[:LOC, hs]) * SCALE).astype(BF16)
        dv_ref[:LOC, hs] = nn(p, g).astype(BF16)
        dq_ref[:LOC, hs] = (nn(k.T, ds).T * SCALE).astype(BF16)

    for s in range(1, 8):
        ring(s)
        if 2 <= s <= 5:
            pl.when(is_hot)(lambda: hot_back(s - 2))
    for h in range(3):
        hs = slice(h * HD, (h + 1) * HD)

        @pl.when(z != owner(h))
        def _():
            for n, part in enumerate((pl.ds(0, 1), pl.ds(1, 2))):
                rc(grads_in.at[h, part], grads_in.at[h, part], gs_s.at[h], gr_r.at[n, h], zup).wait_recv()
            dq_ref[LOC:, hs] = grads_in[h, 0]
            dk_ref[LOC:, hs] = grads_in[h, 1]
            dv_ref[LOC:, hs] = grads_in[h, 2]

        @pl.when(z == owner(h))
        def _():
            dq_ref[LOC:, hs] = hot_grads[z, 0]
            dk_ref[LOC:, hs] = hot_grads[z, 1]
            dv_ref[LOC:, hs] = hot_grads[z, 2]

    for i in range(14):
        og_copy(i).wait_send()
    for i in range(5):
        w_copy(i).wait_send()
    for h in range(3):
        @pl.when(z != owner(h))
        def _():
            to_hot(h, 0).wait_send()
            to_hot(h, 1).wait_send()
            g_to_hot(h).wait_send()

    @pl.when(is_hot)
    def _():
        each_other(lambda c: attn_back(c).wait_send())
        each_other(lambda c: dq_back(c).wait_send())
        each_other(lambda c: dkv_back(c).wait_send())

    for i in range(8):
        half(i).wait_send()
    for s in range(8):
        for j in range(3):
            if s < 7:
                down(s, j).wait_send()
            if s < 6:
                up(s, j).wait_send()
    for i in range(5):
        final(i).wait()
    total = red[z] + half_in[z].astype(F32)
    low, high = total[:40], total[40:]
    for i in range(5):
        came = fin_in[i].astype(F32)
        low, high = low + came[:40], high + came[8:]
    wg_ref[...] = jnp.where(y_hi == 0, low, high)


def local(queries, keys, values, out_grad, out_weight, short_docs, long_docs, block_place):
    vm = pl.BlockSpec(memory_space=pltpu.VMEM)
    hbm = pl.BlockSpec(memory_space=pltpu.HBM)
    dma = pltpu.SemaphoreType.DMA
    dq, dk, dv, wg = pl.pallas_call(
        kernel,
        out_shape=(
            jax.ShapeDtypeStruct((320, 384), BF16),
            jax.ShapeDtypeStruct((320, 384), BF16),
            jax.ShapeDtypeStruct((320, 384), BF16),
            jax.ShapeDtypeStruct((40, 384), F32),
        ),
        in_specs=[hbm] * 8,
        out_specs=(vm,) * 4,
        scratch_shapes=[
            pltpu.VMEM((320, 384), BF16),
            pltpu.VMEM((320, 384), BF16),
            pltpu.VMEM((320, 384), BF16),
            pltpu.VMEM((1, 256), jnp.int32),
            pltpu.VMEM((1, 1024), jnp.int32),
            pltpu.SMEM((1, 16), jnp.int32),
            pltpu.VMEM((8, 320, 320), BF16),
            pltpu.VMEM((8, 2, 160, 320), BF16),
            pltpu.VMEM((4, 640, 384), BF16),
            pltpu.VMEM((3, 3, 64, 128), BF16),
            pltpu.VMEM((3, 64, 128), BF16),
            pltpu.VMEM((16, 3, 64, 128), BF16),
            pltpu.VMEM((16, 64, 128), BF16),
            pltpu.VMEM((128, 1024), BF16),
            pltpu.VMEM((1024, 1024), BF16),
            pltpu.VMEM((128, 1024), F32),
            pltpu.VMEM((16, 64, 128), BF16),
            pltpu.VMEM((16, 3, 64, 128), BF16),
            pltpu.VMEM((2, 1024, 128), F32),
            pltpu.VMEM((3, 64, 128), BF16),
            pltpu.VMEM((3, 3, 64, 128), BF16),
            pltpu.VMEM((320, 384), BF16),
            pltpu.VMEM((3, 128, 256), F32),
            pltpu.VMEM((3, 256, 256), BF16),
            pltpu.VMEM((320, 384), F32),
            pltpu.VMEM((320, 384), BF16),
            pltpu.VMEM((16, 80, 384), BF16),
            pltpu.VMEM((16, 80, 384), BF16),
            pltpu.VMEM((8, 80, 384), BF16),
            pltpu.VMEM((8, 80, 384), BF16),
            pltpu.VMEM((7, 80, 384), BF16),
            pltpu.VMEM((7, 80, 384), BF16),
            pltpu.VMEM((16, 80, 384), F32),
            pltpu.VMEM((80, 384), BF16),
            pltpu.VMEM((5, 48, 384), BF16),
            dma((8,)), dma((14,)), dma((14,)), dma((5,)), dma((5,)),
            dma((3, 2)), dma((3,)), dma((16, 2)), dma((16,)),
            dma((16,)), dma((3,)), dma((2, 16)), dma((2, 3)),
            dma((8,)), dma((8,)), dma((8, 3)), dma((8, 3)), dma((7, 3)), dma((7, 3)), dma((5,)), dma((5,)),
        ],
        compiler_params=pltpu.CompilerParams(
            collective_id=0, has_side_effects=True, vmem_limit_bytes=50 * 1024 * 1024
        ),
        name="attention_grads",
    )(
        *(
            pltpu.with_memory_space_constraint(a, pltpu.HBM)
            for a in (
                queries[0, 0], keys[0, 0], values[0, 0], out_grad[0, 0], out_weight,
                short_docs[0], long_docs, block_place,
            )
        )
    )
    shape = queries.shape
    return dq.reshape(shape), dk.reshape(shape), dv.reshape(shape), wg


def solution(mesh):
    placed = (
        P("dp", "ctx", None, "tp"),
        P("dp", "ctx", None, "tp"),
        P("dp", "ctx", None, "tp"),
        P("dp", "ctx", None, "tp"),
        P("dp", "tp"),
        P("dp", "ctx", None),
        P("dp", None),
        P("dp", None),
    )
    return jax.shard_map(
        local,
        mesh=mesh,
        in_specs=placed,
        out_specs=(
            P("dp", "ctx", None, "tp"),
            P("dp", "ctx", None, "tp"),
            P("dp", "ctx", None, "tp"),
            P(("ctx", "dp"), "tp"),
        ),
        check_vma=False,
    )
```

```python
import math

import jax
import jax.numpy as jnp
from jax import lax
from jax.experimental import pallas as pl
from jax.experimental.pallas import tpu as pltpu
from jax.sharding import PartitionSpec as P

HD = 128
LOC = 256
BLK = 64
NEG = -1e30
OWNERS = ((0, 3), (6, 8), (11, 14))
MESH = pl.DeviceIdType.MESH
F32 = jnp.float32
BF16 = jnp.bfloat16
SCALE = HD**-0.5
C2 = SCALE * math.log2(math.e)


def nn(a, b):
    return lax.dot_general(a, b, (((1,), (0,)), ((), ())), preferred_element_type=F32)


def nt(a, b):
    return lax.dot_general(a, b, (((1,), (1,)), ((), ())), preferred_element_type=F32)


def softmax_t(scores, mask):
    s = jnp.where(mask, scores * C2, NEG)
    top = jnp.max(s, axis=0, keepdims=True)
    p = jnp.exp2(s - top)
    return p * (1.0 / jnp.sum(p, axis=0, keepdims=True))


def kernel(
    q_hbm, k_hbm, v_hbm, og_hbm, w_hbm, sdoc_hbm, ldoc_hbm, place_hbm,
    dq_ref, dk_ref, dv_ref, wg_ref,
    q_ref, k_ref, v_ref, sdoc_ref, ldoc_ref, place_ref,
    og_full, og_t, w_full, stage, gstage, hot_in, hot_g, hot_kt, hot_p, hot_at, hot_attn, hot_grads, hot_acc,
    attn_in, grads_in, attn_all, attn_t, p_short, g_all, half_out, half_in,
    down_out, down_in, up_out, up_in, red, self_out, fin_in,
    in_s, og_s, og_r, w_s, w_r, st_s, gs_s, hin_r, hg_r, ha_s, at_r, ho_s, gr_r,
    half_s, half_r, dn_s, dn_r, up_s, up_r, fin_s, fin_r,
):
    z = lax.axis_index("ctx")
    dp = lax.axis_index("dp")
    tp = lax.axis_index("tp")
    nz = 16
    y_hi, core = dp // 2, dp % 2
    y_lo, x = tp // 4, tp % 4
    row, other = y_lo * 4, (1 - y_lo) * 4
    xr, xl, xo = (x + 1) % 4, (x + 3) % 4, (x + 2) % 4
    dpo = (1 - y_hi) * 2 + core
    sib = y_hi * 2 + 1 - core
    sibo = (1 - y_hi) * 2 + 1 - core
    right, left = {"tp": row + xr}, {"tp": row + xl}
    pair = {"tp": other + x}
    opposite = {"dp": dpo}
    sibling = {"dp": sib}
    zup, zdn = {"ctx": (z + 1) % nz}, {"ctx": (z + nz - 1) % nz}
    zup_o, zdn_o = {"ctx": (z + 1) % nz, "dp": dpo}, {"ctx": (z + nz - 1) % nz, "dp": dpo}
    owners = [jnp.where(core == 0, a, b) for a, b in OWNERS]
    is_hot = (z == owners[0]) | (z == owners[1]) | (z == owners[2])
    hot_h = jnp.where(z == owners[1], 1, jnp.where(z == owners[2], 2, 0))

    def rc(src, dst, ss, rs, dev):
        return pltpu.make_async_remote_copy(
            src_ref=src, dst_ref=dst, send_sem=ss, recv_sem=rs, device_id=dev, device_id_type=MESH
        )

    loads = [
        pltpu.make_async_copy(src, dst, in_s.at[i])
        for i, (src, dst) in enumerate(
            (
                (og_hbm, og_full.at[tp]), (k_hbm, k_ref), (q_hbm, q_ref), (v_hbm, v_ref),
                (w_hbm, w_full.at[dp]), (sdoc_hbm, sdoc_ref), (ldoc_hbm, ldoc_ref), (place_hbm, place_ref),
            )
        )
    ]
    for load in loads:
        load.start()

    bar = pltpu.get_barrier_semaphore()
    for dev in (right, left, pair, opposite, sibling, zup_o, zdn_o):
        pl.semaphore_signal(bar, inc=1, device_id=dev, device_id_type=MESH)

    def greet(i, carry):
        pl.semaphore_signal(bar, inc=1, device_id={"ctx": (z + i) % nz}, device_id_type=MESH)
        return carry

    for dev in (zup, zdn):
        pl.semaphore_signal(bar, inc=1, device_id=dev, device_id_type=MESH)

    @pl.when(is_hot)
    def _():
        lax.fori_loop(1, nz, greet, 0)

    for load in loads:
        load.wait()
    pl.semaphore_wait(bar, 12 - is_hot.astype(jnp.int32))

    lo, hi = pl.ds(0, 160), pl.ds(160, 160)
    og = [
        (tp, lo, right, row + xl),
        (tp, hi, right, row + xl),
        (other + x, lo, right, other + xl),
        (row + xl, lo, right, row + xo),
        (other + xl, lo, right, other + xo),
        (tp, hi, left, row + xr),
        (tp, lo, left, row + xr),
        (other + x, hi, left, other + xr),
        (row + xr, hi, left, row + xo),
        (other + xr, hi, left, other + xo),
        (tp, lo, pair, other + x),
        (tp, hi, pair, other + x),
        (other + x, hi, right, other + xl),
        (other + x, lo, left, other + xr),
    ]

    def og_copy(i):
        slot, rows, dev, _ = og[i]
        there = og_full.at[slot, rows]
        return rc(there, there, og_s.at[i], og_r.at[i], dev)

    def og_wait(i):
        _, rows, dev, slot = og[i]
        here = og_full.at[slot, rows]
        rc(here, here, og_s.at[i], og_r.at[i], dev).wait_recv()

    def turn(slot):
        t = og_full[slot].astype(F32).T.reshape(4, 2, 40, 320)
        og_t[slot, 0] = t[:, 0].reshape(160, 320).astype(BF16)
        og_t[slot, 1] = t[:, 1].reshape(160, 320).astype(BF16)

    wlo, whi, wall = pl.ds(0, 320), pl.ds(320, 320), pl.ds(0, 640)

    def w_copy(i):
        slot, rows, dev = (
            (dp, wlo, opposite), (dp, whi, opposite), (dp, wall, sibling), (dpo, wlo, sibling), (dpo, whi, sibling),
        )[i]
        there = w_full.at[slot, rows]
        return rc(there, there, w_s.at[i], w_r.at[i], dev)

    def w_wait(i):
        slot, rows = ((dpo, wlo), (dpo, whi), (sib, wall), (sibo, wlo), (sibo, whi))[i]
        here = w_full.at[slot, rows]
        rc(here, here, w_s.at[i], w_r.at[i], sibling).wait_recv()

    for i in (10, 0, 5, 11, 1, 6):
        og_copy(i).start()

    def owner(h):
        return owners[h]

    parts = (pl.ds(0, 2), pl.ds(2, 1))

    def to_hot(h, n):
        return rc(
            stage.at[h, parts[n]], hot_in.at[z, parts[n]], st_s.at[h, n], hin_r.at[z, n], {"ctx": owner(h)}
        )

    def g_to_hot(h):
        return rc(gstage.at[h], hot_g.at[z], gs_s.at[h], hg_r.at[z], {"ctx": owner(h)})

    for h in range(3):
        hs = slice(h * HD, (h + 1) * HD)
        stage[h, 0] = q_ref[LOC:, hs]
        stage[h, 1] = k_ref[LOC:, hs]
        stage[h, 2] = v_ref[LOC:, hs]
    for n in range(2):
        for h in range(3):
            @pl.when(z != owner(h))
            def _():
                to_hot(h, n).start()

    for h in range(3):
        @pl.when(z == owner(h))
        def _():
            hot_in[z] = stage[h]

    for i in range(3):
        w_copy(i).start()

    sid = sdoc_ref[...].astype(F32)
    sid_col = jnp.broadcast_to(sid, (HD, LOC)).T
    sid_col = jnp.concatenate([sid_col, sid_col], axis=1)
    kk = lax.broadcasted_iota(jnp.int32, (LOC, LOC), 0)
    qq = lax.broadcasted_iota(jnp.int32, (LOC, LOC), 1)
    smask = (kk <= qq) & (sid_col == sid)

    def short_forward(h):
        hs = slice(h * HD, (h + 1) * HD)
        p = softmax_t(nt(k_ref[:LOC, hs], q_ref[:LOC, hs]), smask).astype(BF16)
        p_short[h] = p
        at = nn(v_ref[:LOC, hs].T, p).astype(BF16).astype(F32)
        attn_t[h] = at
        attn_all[:LOC, hs] = at.T.astype(BF16)

    short_forward(0)
    short_forward(1)
    og_wait(10)
    og_copy(2).start()
    og_wait(11)
    og_copy(7).start()
    og_wait(0)
    og_copy(3).start()
    og_wait(5)
    og_copy(8).start()
    og_copy(12).start()
    og_copy(13).start()
    og_wait(1)
    og_wait(6)
    short_forward(2)
    turn(tp)
    turn(other + x)
    og_wait(2)
    og_copy(4).start()
    og_wait(7)
    og_copy(9).start()

    def each_other(fn):
        def body(i, carry):
            fn((z + i) % nz)
            return carry

        lax.fori_loop(1, nz, body, 0)

    def attn_back(c):
        return rc(hot_attn.at[c], attn_in.at[hot_h], ha_s.at[c], at_r.at[hot_h], {"ctx": c})

    def dq_back(c):
        part = pl.ds(0, 1)
        return rc(hot_grads.at[c, part], grads_in.at[hot_h, part], ho_s.at[0, c], gr_r.at[0, hot_h], {"ctx": c})

    def dkv_back(c):
        part = pl.ds(1, 2)
        return rc(hot_grads.at[c, part], grads_in.at[hot_h, part], ho_s.at[1, c], gr_r.at[1, hot_h], {"ctx": c})

    @pl.when(is_hot)
    def _():
        def hot_wait(n):
            each_other(
                lambda c: rc(
                    hot_in.at[c, parts[n]], hot_in.at[c, parts[n]], st_s.at[0, n], hin_r.at[c, n], zup
                ).wait_recv()
            )

        hot_wait(0)
        lane = lax.broadcasted_iota(jnp.int32, (1, 1024), 1)
        blk = lane // BLK
        place = jnp.zeros((1, 1024), jnp.int32)
        for c in range(nz):
            place = jnp.where(blk == c, place_ref[0, c], place)
        qpos = place * BLK + lane % BLK
        total = jnp.sum(ldoc_ref[...].astype(F32), axis=1, keepdims=True)
        cut = 1024 - total.astype(jnp.int32)
        qlo = jnp.where(qpos >= cut, cut, 0)
        k_all = hot_in[:, 1].reshape(1024, HD)
        spot = lax.broadcasted_iota(jnp.int32, (BLK, 256), 0)
        kpos = jnp.concatenate([spot + place_ref[0, c] * BLK for c in range(nz)], axis=0)

        def weigh(t):
            ts = slice(t * 256, (t + 1) * 256)
            q_t = hot_in[4 * t : 4 * t + 4, 0].reshape(256, HD)
            mask = (kpos <= qpos[:, ts]) & (kpos >= qlo[:, ts])
            hot_p[:, ts] = softmax_t(nt(k_all, q_t), mask).astype(BF16)

        weigh(0)
        weigh(1)
        hot_wait(1)
        v_t = hot_in[:, 2].reshape(1024, HD).T
        for t in range(4):
            ts = slice(t * 256, (t + 1) * 256)
            if t > 1:
                weigh(t)
            at = nn(v_t, hot_p[:, ts]).astype(BF16).astype(F32)
            hot_at[:, ts] = at
            hot_attn[4 * t : 4 * t + 4] = at.T.astype(BF16).reshape(4, BLK, HD)
            for c in range(4 * t, 4 * t + 4):
                @pl.when(z != c)
                def _():
                    attn_back(c).start()
        hot_kt[...] = k_all.T

    turn(row + xl)
    turn(row + xr)
    og_wait(3)
    og_wait(8)
    turn(row + xo)
    og_wait(12)
    turn(other + xl)
    og_wait(13)
    turn(other + xr)
    og_wait(4)
    og_wait(9)
    turn(other + xo)

    def product(slot, k, rows):
        return nn(og_full[2 * slot + k, rows], w_full[slot, k * 320 : k * 320 + 320])

    def products(slot, rows):
        return product(slot, 0, rows) + product(slot, 1, rows)

    short_rows, long_rows = pl.ds(0, LOC), pl.ds(LOC, BLK)

    w_wait(2)
    grad = products(dp, long_rows) + products(sib, long_rows)
    w_wait(0)
    w_copy(3).start()
    w_wait(1)
    w_copy(4).start()
    grad += products(dpo, long_rows)
    w_wait(3)
    w_wait(4)
    grad = (grad + products(sibo, long_rows)).astype(BF16)
    for h in range(3):
        gstage[h] = grad[:, h * HD : (h + 1) * HD]
    for h in range(3):
        @pl.when(z != owner(h))
        def _():
            g_to_hot(h).start()

        @pl.when(z == owner(h))
        def _():
            hot_g[z] = gstage[h]

    for h in range(3):
        hs = slice(h * HD, (h + 1) * HD)

        @pl.when(z != owner(h))
        def _():
            rc(attn_in.at[h], attn_in.at[h], gs_s.at[h], at_r.at[h], zup).wait_recv()
            attn_all[LOC:, hs] = attn_in[h]

        @pl.when(z == owner(h))
        def _():
            attn_all[LOC:, hs] = hot_attn[z]

    sign = 1 - 2 * (z % 2)

    def nth(i):
        step = (i + 1) // 2
        return (z // 2 + 12 + (step if i % 2 == 0 else -step) * sign) % 8

    def half(i):
        there = pl.ds(2 * nth(i), 2)
        return rc(half_out.at[there], half_in.at[there], half_s.at[i], half_r.at[i], sibling)

    def piece(i):
        t = nth(i)
        attn = attn_all[...]
        half_out[pl.ds(2 * t, 2)] = nn(og_t[t, 1 - core], attn).astype(BF16).reshape(2, 80, 384)
        half(i).start()
        red[pl.ds(2 * t, 2)] = nn(og_t[t, core], attn).reshape(2, 80, 384)

    for i in range(4):
        piece(i)

    subs = (pl.ds(0, 32), pl.ds(32, 32), pl.ds(64, 16))

    def down(s, j):
        return rc(down_out.at[s, subs[j]], down_in.at[s, subs[j]], dn_s.at[s, j], dn_r.at[s, j], zdn)

    def up(s, j):
        return rc(up_out.at[s, subs[j]], up_in.at[s, subs[j]], up_s.at[s, j], up_r.at[s, j], zup)

    def mine(c, j):
        return red[c, subs[j]] + half_in[c, subs[j]].astype(F32)

    def ring(s):
        for i in {0: (0, 1), 1: (2, 3), 3: (4, 5), 5: (6, 7)}.get(s, ()):
            half(i).wait_recv()
        for j in range(3):
            v = mine((z + 8 + s) % nz, j)
            if s > 0:
                down(s - 1, j).wait_recv()
                v = v + down_in[s - 1, subs[j]].astype(F32)
            down_out[s, subs[j]] = v.astype(BF16)
            if s < 7:
                down(s, j).start()
                v = mine((z + 7 - s) % nz, j)
                if s > 0:
                    up(s - 1, j).wait_recv()
                    v = v + up_in[s - 1, subs[j]].astype(F32)
                up_out[s, subs[j]] = v.astype(BF16)
                if s < 6:
                    up(s, j).start()
        if s == 5:
            self_out[...] = (red[z] + half_in[z].astype(F32)).astype(BF16)
            final(4).start()
        if s == 6:
            final(2).start()
            final(3).start()
        if s == 7:
            final(0).start()
            final(1).start()

    ours, theirs = (pl.ds(pl.multiple_of(32 * k, 16), 48) for k in (y_hi, 1 - y_hi))

    def final(i):
        src, rows, dev = (
            (down_out.at[7], ours, zdn), (down_out.at[7], theirs, zdn_o),
            (up_out.at[6], ours, zup), (up_out.at[6], theirs, zup_o), (self_out, theirs, opposite),
        )[i]
        return rc(src.at[rows], fin_in.at[i], fin_s.at[i], fin_r.at[i], dev)

    def hot_back(t):
        ts = slice(t * 256, (t + 1) * 256)
        if t == 0:
            each_other(lambda c: rc(hot_g.at[c], hot_g.at[c], gs_s.at[0], hg_r.at[c], zup).wait_recv())
        g = hot_g[4 * t : 4 * t + 4].reshape(256, HD)
        q = hot_in[4 * t : 4 * t + 4, 0].reshape(256, HD)
        delta = jnp.sum(g.T.astype(F32) * hot_at[:, ts], axis=0, keepdims=True)
        p = hot_p[:, ts]
        ds = (p.astype(F32) * (nt(hot_in[:, 2].reshape(1024, HD), g) - delta)).astype(BF16)
        dk = nn(ds, q)
        dv = nn(p, g)
        if t > 0:
            dk += hot_acc[0]
            dv += hot_acc[1]
        dq = nn(hot_kt[...], ds).T * SCALE
        hot_grads[4 * t : 4 * t + 4, 0] = dq.astype(BF16).reshape(4, BLK, HD)
        for c in range(4 * t, 4 * t + 4):
            @pl.when(z != c)
            def _():
                dq_back(c).start()
        if t < 3:
            hot_acc[0] = dk
            hot_acc[1] = dv
        else:
            hot_grads[:, 1] = (dk * SCALE).astype(BF16).reshape(nz, BLK, HD)
            hot_grads[:, 2] = dv.astype(BF16).reshape(nz, BLK, HD)
            each_other(lambda c: dkv_back(c).start())

    ring(0)
    for i in range(4, 8):
        piece(i)

    g_all[...] = (
        (products(dp, short_rows) + products(sib, short_rows)) + (products(dpo, short_rows) + products(sibo, short_rows))
    ).astype(BF16)

    for h in range(3):
        hs = slice(h * HD, (h + 1) * HD)
        g = g_all[:, hs]
        v, k = v_ref[:LOC, hs], k_ref[:LOC, hs]
        delta = jnp.sum(g.T.astype(F32) * attn_t[h], axis=0, keepdims=True)
        p = p_short[h]
        ds = (p.astype(F32) * (nt(v, g) - delta)).astype(BF16)
        dk_ref[:LOC, hs] = (nn(ds, q_ref[:LOC, hs]) * SCALE).astype(BF16)
        dv_ref[:LOC, hs] = nn(p, g).astype(BF16)
        dq_ref[:LOC, hs] = (nn(k.T, ds).T * SCALE).astype(BF16)

    for s in range(1, 8):
        ring(s)
        if 2 <= s <= 5:
            pl.when(is_hot)(lambda: hot_back(s - 2))
    for h in range(3):
        hs = slice(h * HD, (h + 1) * HD)

        @pl.when(z != owner(h))
        def _():
            for n, part in enumerate((pl.ds(0, 1), pl.ds(1, 2))):
                rc(grads_in.at[h, part], grads_in.at[h, part], gs_s.at[h], gr_r.at[n, h], zup).wait_recv()
            dq_ref[LOC:, hs] = grads_in[h, 0]
            dk_ref[LOC:, hs] = grads_in[h, 1]
            dv_ref[LOC:, hs] = grads_in[h, 2]

        @pl.when(z == owner(h))
        def _():
            dq_ref[LOC:, hs] = hot_grads[z, 0]
            dk_ref[LOC:, hs] = hot_grads[z, 1]
            dv_ref[LOC:, hs] = hot_grads[z, 2]

    for i in range(14):
        og_copy(i).wait_send()
    for i in range(5):
        w_copy(i).wait_send()
    for h in range(3):
        @pl.when(z != owner(h))
        def _():
            to_hot(h, 0).wait_send()
            to_hot(h, 1).wait_send()
            g_to_hot(h).wait_send()

    @pl.when(is_hot)
    def _():
        each_other(lambda c: attn_back(c).wait_send())
        each_other(lambda c: dq_back(c).wait_send())
        each_other(lambda c: dkv_back(c).wait_send())

    for i in range(8):
        half(i).wait_send()
    for s in range(8):
        for j in range(3):
            if s < 7:
                down(s, j).wait_send()
            if s < 6:
                up(s, j).wait_send()
    for i in range(5):
        final(i).wait()
    total = red[z] + half_in[z].astype(F32)
    low, high = total[:40], total[40:]
    for i in range(5):
        came = fin_in[i].astype(F32)
        low, high = low + came[:40], high + came[8:]
    wg_ref[...] = jnp.where(y_hi == 0, low, high)


def local(queries, keys, values, out_grad, out_weight, short_docs, long_docs, block_place):
    vm = pl.BlockSpec(memory_space=pltpu.VMEM)
    hbm = pl.BlockSpec(memory_space=pltpu.HBM)
    dma = pltpu.SemaphoreType.DMA
    dq, dk, dv, wg = pl.pallas_call(
        kernel,
        out_shape=(
            jax.ShapeDtypeStruct((320, 384), BF16),
            jax.ShapeDtypeStruct((320, 384), BF16),
            jax.ShapeDtypeStruct((320, 384), BF16),
            jax.ShapeDtypeStruct((40, 384), F32),
        ),
        in_specs=[hbm] * 8,
        out_specs=(vm,) * 4,
        scratch_shapes=[
            pltpu.VMEM((320, 384), BF16),
            pltpu.VMEM((320, 384), BF16),
            pltpu.VMEM((320, 384), BF16),
            pltpu.VMEM((1, 256), jnp.int32),
            pltpu.VMEM((1, 1024), jnp.int32),
            pltpu.SMEM((1, 16), jnp.int32),
            pltpu.VMEM((8, 320, 320), BF16),
            pltpu.VMEM((8, 2, 160, 320), BF16),
            pltpu.VMEM((4, 640, 384), BF16),
            pltpu.VMEM((3, 3, 64, 128), BF16),
            pltpu.VMEM((3, 64, 128), BF16),
            pltpu.VMEM((16, 3, 64, 128), BF16),
            pltpu.VMEM((16, 64, 128), BF16),
            pltpu.VMEM((128, 1024), BF16),
            pltpu.VMEM((1024, 1024), BF16),
            pltpu.VMEM((128, 1024), F32),
            pltpu.VMEM((16, 64, 128), BF16),
            pltpu.VMEM((16, 3, 64, 128), BF16),
            pltpu.VMEM((2, 1024, 128), F32),
            pltpu.VMEM((3, 64, 128), BF16),
            pltpu.VMEM((3, 3, 64, 128), BF16),
            pltpu.VMEM((320, 384), BF16),
            pltpu.VMEM((3, 128, 256), F32),
            pltpu.VMEM((3, 256, 256), BF16),
            pltpu.VMEM((256, 384), BF16),
            pltpu.VMEM((16, 80, 384), BF16),
            pltpu.VMEM((16, 80, 384), BF16),
            pltpu.VMEM((8, 80, 384), BF16),
            pltpu.VMEM((8, 80, 384), BF16),
            pltpu.VMEM((7, 80, 384), BF16),
            pltpu.VMEM((7, 80, 384), BF16),
            pltpu.VMEM((16, 80, 384), F32),
            pltpu.VMEM((80, 384), BF16),
            pltpu.VMEM((5, 48, 384), BF16),
            dma((8,)), dma((14,)), dma((14,)), dma((5,)), dma((5,)),
            dma((3, 2)), dma((3,)), dma((16, 2)), dma((16,)),
            dma((16,)), dma((3,)), dma((2, 16)), dma((2, 3)),
            dma((8,)), dma((8,)), dma((8, 3)), dma((8, 3)), dma((7, 3)), dma((7, 3)), dma((5,)), dma((5,)),
        ],
        compiler_params=pltpu.CompilerParams(
            collective_id=0, has_side_effects=True, vmem_limit_bytes=50 * 1024 * 1024
        ),
        name="attention_grads",
    )(
        *(
            pltpu.with_memory_space_constraint(a, pltpu.HBM)
            for a in (
                queries[0, 0], keys[0, 0], values[0, 0], out_grad[0, 0], out_weight,
                short_docs[0], long_docs, block_place,
            )
        )
    )
    shape = queries.shape
    return dq.reshape(shape), dk.reshape(shape), dv.reshape(shape), wg


def solution(mesh):
    placed = (
        P("dp", "ctx", None, "tp"),
        P("dp", "ctx", None, "tp"),
        P("dp", "ctx", None, "tp"),
        P("dp", "ctx", None, "tp"),
        P("dp", "tp"),
        P("dp", "ctx", None),
        P("dp", None),
        P("dp", None),
    )
    return jax.shard_map(
        local,
        mesh=mesh,
        in_specs=placed,
        out_specs=(
            P("dp", "ctx", None, "tp"),
            P("dp", "ctx", None, "tp"),
            P("dp", "ctx", None, "tp"),
            P(("ctx", "dp"), "tp"),
        ),
        check_vma=False,
    )
```
